128 devices in a mesh: depth: 4 (over z_hi, core), row: 8 (over x, z_lo), col: 4 (over y).
Axes of the slice: x: 4, y: 4, z: 4 (z_hi: 2, z_lo: 2; z = z_hi * 2 + z_lo), core: 2. Of those that a mesh axis runs over, the one named last changes fastest.
Arguments:
- tokens_in: bfloat16 [4096, 4096], P(('depth', 'row'), 'col'), may hold values from -6 to 6
- grad_out: bfloat16 [4096, 4096], P(('depth', 'row'), 'col'), may hold values from -6 to 6
- gate_pre: bfloat16 [4096, 14336], P(('depth', 'col'), 'row'), may hold values from -6 to 6
- up_pre: bfloat16 [4096, 14336], P(('depth', 'col'), 'row'), may hold values from -6 to 6
- gate_weight: bfloat16 [4096, 14336], P(('col', 'depth'), 'row'), may hold values from -0.09375 to 0.09375
- up_weight: bfloat16 [4096, 14336], P(('col', 'depth'), 'row'), may hold values from -0.09375 to 0.09375
- down_weight: bfloat16 [14336, 4096], P('row', ('col', 'depth')), may hold values from -0.046875 to 0.046875
Outputs:
- grad_in: bfloat16 [4096, 4096], P(('depth', 'row'), 'col')
- grad_gate_w: bfloat16 [4096, 14336], P(('col', 'depth'), 'row')
- grad_up_w: bfloat16 [4096, 14336], P(('col', 'depth'), 'row')
- grad_down_w: bfloat16 [14336, 4096], P('row', ('col', 'depth'))
The draws below stay inside these ranges and needn't reach their ends.
All inputs are finite; a program needn't handle non-finite values.
Results may differ from the reference program's by a relative error of at most 0.025.
Values may be sent and summed in bfloat16 or wider, within the bound.
A program may use at most 128 MiB of HBM per device.

```python
import math
import jax
import jax.numpy as jnp
from jax import lax

D = 4096
FF = 14336
TOK_GROUP = 1024
TOKENS = 4096
N_DEPTH = 4


def spiked(array, rng, source, target, parts, factor):
    owner, partner = [(jnp.arange(array.shape[axis_at]) // (array.shape[axis_at] // parts)).reshape([-1 if axis == axis_at else 1 for axis in range(array.ndim)]) for axis_at in (source, target)]
    chosen = jax.random.permutation(rng, parts)[partner]
    strong = (owner == chosen) | (owner == (partner + parts // 2) % parts)
    return jnp.where(strong, factor * array, array)


def block_levels(own_key, dims, shards, smallest, largest):
    def one(axis_at, shards_of):
        heights = jax.random.uniform(jax.random.fold_in(jax.random.fold_in(own_key, 6), axis_at), (shards_of,), jnp.float32, smallest / len(shards), largest / len(shards))
        return jnp.repeat(jnp.exp(heights), dims[axis_at] // shards_of).reshape((-1,) + (1,) * (len(dims) - axis_at - 1))

    loudness = one(*shards[0])
    for cut in shards[1:]:
        loudness = loudness * one(*cut)
    return loudness


def gaussian(key, extent, width, limit, cuts=(), kind=jnp.bfloat16):
    loudness = block_levels(key, extent, cuts, -0.22, 0.18) if cuts else 1.0
    values = jax.random.normal(key, extent, jnp.float32) * width * loudness
    return jnp.minimum(jnp.maximum(values, -limit), limit).astype(kind)


def heavy_noise(rng, shape, width, most, pieces, heavy, held_as=jnp.bfloat16):
    result = width * jax.random.normal(rng, shape, jnp.float32)
    if pieces:
        result = result * block_levels(rng, shape, pieces, -0.22, 0.18)
    return jnp.clip(spiked(result, jax.random.fold_in(rng, 3), *heavy), -most, most).astype(held_as)


def setup_inputs(seed: int = 0) -> dict:
    seeds = jax.random.split(jax.random.key(seed), 8)
    tokens_in = gaussian(seeds[0], (TOKENS, D), 1.0, 6.0, ((0, 32), (1, 4)))
    grad_out = heavy_noise(seeds[1], (TOKENS, D), 1.0, 6.0, ((0, 32), (1, 4)), (0, 1, 32, 2.75))
    gate_pre = gaussian(seeds[2], (TOKENS, FF), 1.5, 6.0, ((0, 16), (1, 8)))
    up_pre = gaussian(seeds[3], (TOKENS, FF), 1.0, 6.0, ((0, 16), (1, 8)))
    gate_weight = gaussian(seeds[4], (D, FF), D ** -0.5, 0.09375, ((0, 16), (1, 8)))
    up_weight = gaussian(seeds[5], (D, FF), D ** -0.5, 0.09375, ((0, 16), (1, 8)))
    down_weight = gaussian(seeds[6], (FF, D), FF ** -0.5, 0.046875, ((0, 8), (1, 16)))
    return {"tokens_in": tokens_in, "grad_out": grad_out, "gate_pre": gate_pre, "up_pre": up_pre, "gate_weight": gate_weight, "up_weight": up_weight, "down_weight": down_weight}


def reference(tokens_in, grad_out, gate_pre, up_pre, gate_weight, up_weight, down_weight):
    hidden_grad = jnp.dot(grad_out, down_weight.T, preferred_element_type=jnp.float32)
    gate_value = gate_pre.astype(jnp.float32)
    up_value = up_pre.astype(jnp.float32)
    sigmoid = jax.nn.sigmoid(gate_value)
    swish_value = gate_value * sigmoid
    activ = (swish_value * up_value).astype(jnp.bfloat16)
    grad_gate = (hidden_grad * up_value * sigmoid * (1.0 + gate_value * (1.0 - sigmoid))).astype(jnp.bfloat16)
    grad_up = (hidden_grad * swish_value).astype(jnp.bfloat16)
    grad_in = jnp.dot(grad_gate, gate_weight.T, preferred_element_type=jnp.float32)
    grad_in = grad_in + jnp.dot(grad_up, up_weight.T, preferred_element_type=jnp.float32)
    total_gate = jnp.zeros((D, FF), jnp.float32)
    total_up = jnp.zeros((D, FF), jnp.float32)
    total_down = jnp.zeros((FF, D), jnp.float32)
    for group in range(N_DEPTH):
        first_row = group * TOK_GROUP
        last_row = first_row + TOK_GROUP
        token_rows = tokens_in[first_row:last_row]
        part_gate = jnp.dot(token_rows.T, grad_gate[first_row:last_row], preferred_element_type=jnp.float32).astype(jnp.bfloat16)
        part_up = jnp.dot(token_rows.T, grad_up[first_row:last_row], preferred_element_type=jnp.float32).astype(jnp.bfloat16)
        part_down = jnp.dot(activ[first_row:last_row].T, grad_out[first_row:last_row], preferred_element_type=jnp.float32).astype(jnp.bfloat16)
        part_gate, part_up, part_down = lax.optimization_barrier((part_gate, part_up, part_down))
        total_gate = total_gate + part_gate.astype(jnp.float32)
        total_up = total_up + part_up.astype(jnp.float32)
        total_down = total_down + part_down.astype(jnp.float32)
    grad_scale = 1.0 / math.sqrt(TOKENS)
    return (grad_in.astype(jnp.bfloat16), (total_gate * grad_scale).astype(jnp.bfloat16), (total_up * grad_scale).astype(jnp.bfloat16), (total_down * grad_scale).astype(jnp.bfloat16))
```

```python
import functools
import math

import jax
import jax.numpy as jnp
from jax import lax
from jax.experimental import pallas as pl
from jax.experimental.pallas import tpu as pltpu
from jax.sharding import PartitionSpec as P

MESH = pl.DeviceIdType.MESH
BF = jnp.bfloat16
F32 = jnp.float32
NC = 7
CH = 256
AHEAD = 3


def dot_nt(a, b):
    return lax.dot_general(a, b, (((1,), (1,)), ((), ())), preferred_element_type=F32)


def dot_nn(a, b):
    return lax.dot_general(a, b, (((1,), (0,)), ((), ())), preferred_element_type=F32)


def remote(src, dst, ssem, rsem, dev):
    return pltpu.make_async_remote_copy(
        src_ref=src, dst_ref=dst, send_sem=ssem, recv_sem=rsem, device_id=dev, device_id_type=MESH
    )


def kernel(
    scale,
    tok_in, go_in, gp_in, up_in, gw_in, uw_in, dw_in,
    gin_out, ggw_out, guw_out, gdw_out, tkl,
    go, tkt, dw, wgu, gpu, rs1s, rs1r, rs2s, rs2r, nb, own, hid, ggu, ac, act, acc, pin, gr,
    cs, cr, opart, zs, zr, oq,
    loc, go_s, go_r, tk_s, tk_r, dw_s, dw_r, wg_s, wg_r, gp_s, gp_r,
    rs1_s, rs1_m, rs2_s, rs2_m, ag1_s, ag1_m, ag2_s, ag2_m, c_s, c_m, z_s, z_m, gi_s, gi_m,
):
    dep = lax.axis_index("depth")
    row = lax.axis_index("row")
    y = lax.axis_index("col")
    zh, co = dep // 2, dep % 2
    x, zl = row // 2, row % 2
    yp, ym, yo = (y + 1) % 4, (y + 3) % 4, (y + 2) % 4
    up_dev = (dep, row, yp)
    dn_dev = (dep, row, ym)
    zhi_dep = (1 - zh) * 2 + co
    core_dep = zh * 2 + (1 - co)
    zhi_dev = (zhi_dep, row, y)
    core_dev = (core_dep, row, y)
    zlo_row = x * 2 + (1 - zl)
    zlo_dev = (dep, zlo_row, y)
    xs = [((x + d) % 4) * 2 + zl for d in (1, 3, 2)]
    x_dev = [(dep, r, y) for r in xs]

    def wait_recv(ref, sem, dev):
        remote(ref, ref, sem, sem, dev).wait_recv()

    def wait_send(ref, sem, dev):
        remote(ref, ref, sem, sem, dev).wait_send()

    def rows(r, n):
        return pl.ds(pl.multiple_of(r * n, n), n)

    l_go = pltpu.make_async_copy(go_in, go.at[rows(row, 128)], loc.at[0])
    l_dw = pltpu.make_async_copy(dw_in, dw.at[:, rows(dep, 256)], loc.at[1])
    l_tk = pltpu.make_async_copy(tok_in, tkl.at[rows(row, 128)], loc.at[2])
    l_go.start()
    l_dw.start()

    def l_gp(j):
        c = pl.ds(j * CH, CH)
        return (
            pltpu.make_async_copy(gp_in.at[:, c], gpu.at[j, y, 0], loc.at[4 + j]),
            pltpu.make_async_copy(up_in.at[:, c], gpu.at[j, y, 1], loc.at[11 + j]),
        )

    def l_wg(j):
        c = pl.ds(j * CH, CH)
        return (
            pltpu.make_async_copy(gw_in.at[:, c], wgu.at[j, rows(dep, 256), 0:CH], loc.at[18 + j]),
            pltpu.make_async_copy(
                uw_in.at[:, c], wgu.at[j, rows(dep, 256), CH : 2 * CH], loc.at[25 + j]
            ),
        )

    for j in range(NC):
        for c in l_gp(j):
            c.start()
    for j in range(NC):
        for c in l_wg(j):
            c.start()
    l_tk.start()

    barrier = pltpu.get_barrier_semaphore()
    peers = [up_dev, dn_dev, zhi_dev, core_dev]
    for d in range(1, 8):
        peers.append((dep, (row + d) % 8, y))
    for dev in peers:
        pl.semaphore_signal(barrier, inc=1, device_id=dev, device_id_type=MESH)
    pl.semaphore_wait(barrier, len(peers))

    def row_sends(buf, ssem, rsem, r, which):
        ref = buf.at[rows(r, 128)]
        cps = [remote(ref, ref, ssem.at[which, i], rsem.at[r], x_dev[i]) for i in range(3)]
        if which == 0:
            cps.append(remote(ref, ref, ssem.at[0, 3], rsem.at[r], zlo_dev))
        return cps

    def dw_ref(p):
        return dw.at[:, rows(p, 256)]

    def wg_ref(j, p):
        return wgu.at[j, rows(p, 256)]

    def gp_step1(j):
        ref = gpu.at[j, y]
        return (
            remote(ref, ref, gp_s.at[j, 0], gp_r.at[j, 0], up_dev),
            remote(ref, ref, gp_s.at[j, 1], gp_r.at[j, 1], dn_dev),
        )

    def gp_step2(j):
        a, b = gpu.at[j, ym, 0], gpu.at[j, yp, 1]
        return (
            remote(a, a, gp_s.at[j, 2], gp_r.at[j, 2], up_dev),
            remote(b, b, gp_s.at[j, 3], gp_r.at[j, 3], dn_dev),
        )

    def gp_relay(j):
        f, s = gp_step2(j)
        wait_recv(gpu.at[j, ym], gp_r.at[j, 0], dn_dev)
        f.start()
        wait_recv(gpu.at[j, yp], gp_r.at[j, 1], up_dev)
        s.start()

    def wg_send(j):
        ref = wg_ref(j, dep)
        return (
            remote(ref, ref, wg_s.at[j, 0], wg_r.at[j, 0], zhi_dev),
            remote(ref, ref, wg_s.at[j, 1], wg_r.at[j, 1], core_dev),
        )

    def wg_fwd(j):
        ref = wg_ref(j, zhi_dep)
        return remote(ref, ref, wg_s.at[j, 2], wg_r.at[j, 2], core_dev)

    l_go.wait()
    for c in row_sends(go, go_s, go_r, row, 0):
        c.start()
    l_dw.wait()
    ref = dw_ref(dep)
    dw_a = remote(ref, ref, dw_s.at[0], dw_r.at[0], zhi_dev)
    dw_b = remote(ref, ref, dw_s.at[1], dw_r.at[1], core_dev)
    dw_a.start()
    dw_b.start()
    for j in range(NC):
        for c in l_gp(j):
            c.wait()
        if j < AHEAD:
            for c in gp_step1(j):
                c.start()
    wait_recv(go.at[rows(zlo_row, 128)], go_r.at[zlo_row], zlo_dev)
    for c in row_sends(go, go_s, go_r, zlo_row, 1):
        c.start()
    for j in range(NC):
        for c in l_wg(j):
            c.wait()
    l_tk.wait()
    acc[...] = jnp.zeros_like(acc)
    for j in range(AHEAD):
        gp_relay(j)
        if j == 1:
            for c in row_sends(tkl, tk_s, tk_r, row, 0):
                c.start()
    wait_recv(dw_ref(zhi_dep), dw_r.at[0], zhi_dev)
    ref = dw_ref(zhi_dep)
    dw_c = remote(ref, ref, dw_s.at[2], dw_r.at[2], core_dev)
    dw_c.start()
    for j in range(2):
        for c in wg_send(j):
            c.start()
    wait_recv(dw_ref(core_dep), dw_r.at[1], core_dev)
    for i in range(3):
        wait_recv(go.at[rows(xs[i], 128)], go_r.at[xs[i]], x_dev[i])
    for d in (1, 3, 2):
        r = ((x + d) % 4) * 2 + (1 - zl)
        wait_recv(go.at[rows(r, 128)], go_r.at[r], zlo_dev)
    wait_recv(dw_ref((1 - zh) * 2 + (1 - co)), dw_r.at[2], core_dev)

    def rs1_copies(k):
        return (
            remote(rs1s.at[k, 0:128], rs1r.at[k, 0], rs1_s.at[k, 0], rs1_m.at[k, 0], up_dev),
            remote(rs1s.at[k, 128:256], rs1r.at[k, 1], rs1_s.at[k, 1], rs1_m.at[k, 1], dn_dev),
        )

    def rs2_copies(k):
        return (
            remote(rs2s.at[k, 0], rs2r.at[k, 0], rs2_s.at[k, 0], rs2_m.at[k, 0], up_dev),
            remote(rs2s.at[k, 1], rs2r.at[k, 1], rs2_s.at[k, 1], rs2_m.at[k, 1], dn_dev),
        )

    def ag1_copies(k):
        ref = hid.at[k, y]
        return (
            remote(ref, ref, ag1_s.at[k, 0], ag1_m.at[k, 0], up_dev),
            remote(ref, ref, ag1_s.at[k, 1], ag1_m.at[k, 1], dn_dev),
        )

    def ag2_copies(k):
        a, b = hid.at[k, ym, 0:128], hid.at[k, yp, 128:256]
        return (
            remote(a, a, ag2_s.at[k, 0], ag2_m.at[k, 0], up_dev),
            remote(b, b, ag2_s.at[k, 1], ag2_m.at[k, 1], dn_dev),
        )

    def stage_a(k):
        w = dw[rows(k, CH), :]

        def part(q):
            return dot_nt(go[rows(q, 256), :], w)

        rs1s[k] = part(yo).astype(BF)
        for c in rs1_copies(k):
            c.start()
        nb[0] = part(yp)
        nb[1] = part(ym)
        own[k % 2] = part(y)

    def stage_b(k):
        wait_recv(rs1r.at[k, 0], rs1_m.at[k, 0], dn_dev)
        f, s = rs2_copies(k)
        rs2s[k, 0, 0:128] = (nb[0, 0:128] + rs1r[k, 0].astype(F32)).astype(BF)
        rs2s[k, 0, 128:256] = nb[0, 128:256].astype(BF)
        f.start()
        wait_recv(rs1r.at[k, 1], rs1_m.at[k, 1], up_dev)
        rs2s[k, 1, 0:128] = nb[1, 0:128].astype(BF)
        rs2s[k, 1, 128:256] = (nb[1, 128:256] + rs1r[k, 1].astype(F32)).astype(BF)
        s.start()

    def stage_c(k):
        wait_recv(rs2r.at[k, 0], rs2_m.at[k, 0], dn_dev)
        wait_recv(rs2r.at[k, 1], rs2_m.at[k, 1], up_dev)
        hid[k, y] = (own[k % 2] + rs2r[k, 0].astype(F32) + rs2r[k, 1].astype(F32)).astype(BF)
        for c in ag1_copies(k):
            c.start()

    def stage_d(k):
        f, s = ag2_copies(k)
        wait_recv(hid.at[k, ym], ag1_m.at[k, 0], dn_dev)
        f.start()
        wait_recv(hid.at[k, yp], ag1_m.at[k, 1], up_dev)
        s.start()

    def core_copy(j):
        return remote(cs.at[j % 2], cr.at[j], c_s.at[j], c_m.at[j], core_dev)

    def z_copy(j):
        return remote(zs.at[j % 2], zr.at[j], z_s.at[j], z_m.at[j], zhi_dev)

    def grad_parts(p):
        a = dot_nn(tkt[rows(p, 256), :], ggu[...])
        b = dot_nn(act[...], go[:, rows(p, 256)])
        return a, b

    def stage_e1(j):
        wait_recv(gpu.at[j, yo, 0], gp_r.at[j, 2], dn_dev)
        wait_recv(gpu.at[j, yo, 1], gp_r.at[j, 3], up_dev)
        wait_recv(hid.at[j, yo, 0:128], ag2_m.at[j, 0], dn_dev)
        wait_recv(hid.at[j, yo, 128:256], ag2_m.at[j, 1], up_dev)

        @pl.loop(0, 16)
        def _(i):
            c = i // 4
            r = pl.ds(pl.multiple_of((i % 4) * 64, 64), 64)
            o = pl.ds(pl.multiple_of(i * 64, 64), 64)
            h = hid[j, c, r, :].astype(F32)
            g = gpu[j, c, 0, r, :].astype(F32)
            u = gpu[j, c, 1, r, :].astype(F32)
            s = jax.nn.sigmoid(g)
            w = g * s
            ac[o, :] = (w * u).astype(BF)
            ggu[o, 0:CH] = (h * u * s * (1.0 + g * (1.0 - s))).astype(BF)
            ggu[o, CH : 2 * CH] = (h * w).astype(BF)

        for c in range(4):
            act[:, c * 256 : (c + 1) * 256] = ac[c * 256 : (c + 1) * 256, :].T

        @pl.when(j >= 2)
        def _():
            core_copy(j - 2).wait_send()

        @pl.loop(0, 2)
        def _(h):
            a, b = grad_parts(h * 2 + (1 - co))
            cs[j % 2, h, :, 0 : 2 * CH] = a.astype(BF)
            cs[j % 2, h, :, 2 * CH : 3 * CH] = b.astype(BF)

        core_copy(j).start()

        @pl.loop(0, 2)
        def _(h):
            a, b = grad_parts(h * 2 + co)
            opart[h, :, 0 : 2 * CH] = a
            opart[h, :, 2 * CH : 3 * CH] = b

    def gi_copy(d):
        r = (row + d) % 8
        return remote(
            pin.at[rows(r, 128)], gr.at[row], gi_s.at[d], gi_m.at[row], (dep, r, y)
        )

    def stage_e2(j):
        wait_recv(wg_ref(j, zhi_dep), wg_r.at[j, 0], zhi_dev)
        wg_fwd(j).start()
        wait_recv(wg_ref(j, core_dep), wg_r.at[j, 1], core_dev)
        wait_recv(wg_ref(j, (1 - zh) * 2 + (1 - co)), wg_r.at[j, 2], core_dev)

        @pl.loop(0, 4)
        def _(q):
            o = rows(q, 256)
            acc[o, :] += dot_nt(ggu[o, :], wgu[j])

    def stage_f(j):
        @pl.when(j >= 2)
        def _():
            z_copy(j - 2).wait_send()

        wait_recv(cr.at[j], c_m.at[j], core_dev)
        zs[j % 2] = (opart[1 - zh] + cr[j, 1 - zh].astype(F32)).astype(BF)
        z_copy(j).start()
        oq[j % 2] = opart[zh] + cr[j, zh].astype(F32)

    def stage_g(j):
        wait_recv(zr.at[j], z_m.at[j], zhi_dev)
        t = (oq[j % 2] + zr[j].astype(F32)) * scale
        c = rows(j, CH)
        ggw_out[:, c] = t[:, 0:CH].astype(BF)
        guw_out[:, c] = t[:, CH : 2 * CH].astype(BF)
        gdw_out[c, :] = t[:, 2 * CH : 3 * CH].astype(BF)

    def when(cond):
        return pl.when(cond)

    def body(k, carry):
        @when(k < NC)
        def _():
            stage_a(k)

        @when((k >= 1) & (k < NC + 1))
        def _():
            stage_c(k - 1)

        @when((k >= AHEAD - 2) & (k + 2 < NC))
        def _():
            for c in gp_step1(k + 2):
                c.start()

        @when(k + 2 < NC)
        def _():
            for c in wg_send(k + 2):
                c.start()

        @when(k == 0)
        def _():
            wait_recv(tkl.at[rows(zlo_row, 128)], tk_r.at[zlo_row], zlo_dev)
            for c in row_sends(tkl, tk_s, tk_r, zlo_row, 1):
                c.start()

        @when((k >= 3) & (k < NC + 3))
        def _():
            stage_f(k - 3)

        @when((k >= 2) & (k < NC + 2))
        def _():
            stage_e1(k - 2)

        @when(k < NC)
        def _():
            stage_b(k)

        @when((k >= 1) & (k < NC + 1))
        def _():
            stage_d(k - 1)

        @when((k >= AHEAD - 2) & (k + 2 < NC))
        def _():
            gp_relay(k + 2)

        @when(k == 1)
        def _():
            for i in range(3):
                wait_recv(tkl.at[rows(xs[i], 128)], tk_r.at[xs[i]], x_dev[i])
            for d in (1, 3, 2):
                r = ((x + d) % 4) * 2 + (1 - zl)
                wait_recv(tkl.at[rows(r, 128)], tk_r.at[r], zlo_dev)
            cp = pltpu.make_async_copy(tkl, pin, loc.at[3])
            cp.start()
            cp.wait()

            @pl.loop(0, 4)
            def _(q):
                o = rows(q, 256)
                tkt[:, o] = pin[o, :].T

        @when((k >= 2) & (k < NC + 2))
        def _():
            stage_e2(k - 2)

        @when(k == NC + 1)
        def _():
            pin[...] = acc[...].astype(BF)
            for d in (4, 3, 5, 2, 6, 1, 7):
                gi_copy(d).start()

        @when(k >= 4)
        def _():
            stage_g(k - 4)

        return carry

    lax.fori_loop(0, NC + 4, body, 0)

    total = acc[rows(row, 128), :]
    for d in (1, 7, 2, 6, 3, 5, 4):
        r = (row + d) % 8
        wait_recv(gr.at[r], gi_m.at[r], (dep, r, y))
        total = total + gr[r].astype(F32)
    gin_out[...] = total.astype(BF)

    for c in row_sends(go, go_s, go_r, row, 0) + row_sends(go, go_s, go_r, zlo_row, 1):
        c.wait_send()
    for c in row_sends(tkl, tk_s, tk_r, row, 0) + row_sends(tkl, tk_s, tk_r, zlo_row, 1):
        c.wait_send()
    dw_a.wait_send()
    dw_b.wait_send()
    dw_c.wait_send()
    for d in range(1, 8):
        gi_copy(d).wait_send()

    def drain(j, carry):
        for c in (*gp_step1(j), *gp_step2(j), *wg_send(j), wg_fwd(j), *rs1_copies(j)):
            c.wait_send()
        for c in (*rs2_copies(j), *ag1_copies(j), *ag2_copies(j)):
            c.wait_send()

        @pl.when(j >= NC - 2)
        def _():
            core_copy(j).wait_send()
            z_copy(j).wait_send()

        return carry

    lax.fori_loop(0, NC, drain, 0)


def shards(tokens_in, grad_out, gate_pre, up_pre, gate_weight, up_weight, down_weight):
    scale = 1.0 / math.sqrt(4096.0)
    dma = pltpu.SemaphoreType.DMA
    vm = pltpu.VMEM
    hbm = pl.BlockSpec(memory_space=pl.ANY)
    vmem = pl.BlockSpec(memory_space=pltpu.VMEM)
    outs = pl.pallas_call(
        functools.partial(kernel, scale),
        out_shape=[
            jax.ShapeDtypeStruct((128, 1024), BF),
            jax.ShapeDtypeStruct((256, 1792), BF),
            jax.ShapeDtypeStruct((256, 1792), BF),
            jax.ShapeDtypeStruct((1792, 256), BF),
            jax.ShapeDtypeStruct((1024, 1024), BF),
        ],
        in_specs=[hbm] * 7,
        out_specs=[vmem] * 4 + [hbm],
        scratch_shapes=[
            vm((1024, 1024), BF),
            vm((1024, 1024), BF),
            vm((1792, 1024), BF),
            vm((NC, 1024, 2 * CH), BF),
            vm((NC, 4, 2, 256, CH), BF),
            vm((NC, 256, CH), BF),
            vm((NC, 2, 128, CH), BF),
            vm((NC, 2, 256, CH), BF),
            vm((NC, 2, 256, CH), BF),
            vm((2, 256, CH), F32),
            vm((2, 256, CH), F32),
            vm((NC, 4, 256, CH), BF),
            vm((1024, 2 * CH), BF),
            vm((1024, CH), BF),
            vm((CH, 1024), BF),
            vm((1024, 1024), F32),
            vm((1024, 1024), BF),
            vm((8, 128, 1024), BF),
            vm((2, 2, 256, 3 * CH), BF),
            vm((NC, 2, 256, 3 * CH), BF),
            vm((2, 256, 3 * CH), F32),
            vm((2, 256, 3 * CH), BF),
            vm((NC, 256, 3 * CH), BF),
            vm((2, 256, 3 * CH), F32),
            dma((32,)),
            dma((2, 4)), dma((8,)),
            dma((2, 4)), dma((8,)),
            dma((3,)), dma((3,)),
            dma((NC, 3)), dma((NC, 3)),
            dma((NC, 4)), dma((NC, 4)),
            dma((NC, 2)), dma((NC, 2)),
            dma((NC, 2)), dma((NC, 2)),
            dma((NC, 2)), dma((NC, 2)),
            dma((NC, 2)), dma((NC, 2)),
            dma((NC,)), dma((NC,)),
            dma((NC,)), dma((NC,)),
            dma((8,)), dma((8,)),
        ],
        compiler_params=pltpu.CompilerParams(
            collective_id=0, has_side_effects=True, vmem_limit_bytes=62 * 2**20
        ),
        cost_estimate=pl.CostEstimate(
            flops=22_500_000_000, bytes_accessed=20_000_000, transcendentals=2_000_000
        ),
        name="swiglu_backward",
    )(tokens_in, grad_out, gate_pre, up_pre, gate_weight, up_weight, down_weight)
    return tuple(outs[:4])


def solution(mesh):
    return jax.shard_map(
        shards,
        mesh=mesh,
        in_specs=(
            P(("depth", "row"), "col"),
            P(("depth", "row"), "col"),
            P(("depth", "col"), "row"),
            P(("depth", "col"), "row"),
            P(("col", "depth"), "row"),
            P(("col", "depth"), "row"),
            P("row", ("col", "depth")),
        ),
        out_specs=(
            P(("depth", "row"), "col"),
            P(("col", "depth"), "row"),
            P(("col", "depth"), "row"),
            P("row", ("col", "depth")),
        ),
        check_vma=False,
    )
```

```python
import functools
import math

import jax
import jax.numpy as jnp
from jax import lax
from jax.experimental import pallas as pl
from jax.experimental.pallas import tpu as pltpu
from jax.sharding import PartitionSpec as P

MESH = pl.DeviceIdType.MESH
BF = jnp.bfloat16
F32 = jnp.float32
NC = 7
CH = 256
AHEAD = 4


def dot_nt(a, b):
    return lax.dot_general(a, b, (((1,), (1,)), ((), ())), preferred_element_type=F32)


def dot_nn(a, b):
    return lax.dot_general(a, b, (((1,), (0,)), ((), ())), preferred_element_type=F32)


def remote(src, dst, ssem, rsem, dev):
    return pltpu.make_async_remote_copy(
        src_ref=src, dst_ref=dst, send_sem=ssem, recv_sem=rsem, device_id=dev, device_id_type=MESH
    )


def kernel(
    scale,
    tok_in, go_in, gp_in, up_in, gw_in, uw_in, dw_in,
    gin_out, ggw_out, guw_out, gdw_out,
    go, tkt, dw, wgu, gpu, rs1s, rs1r, rs2s, rs2r, nb, own, hid, ggu, ac, act, acc, pin, g1, g2, gs, gz,
    cs, cr, opart, zs, zr, oq,
    loc, go_s, go_r, tk_s, tk_r, dw_s, dw_r, wg_s, wg_r, gp_s, gp_r,
    rs1_s, rs1_m, rs2_s, rs2_m, ag1_s, ag1_m, ag2_s, ag2_m, c_s, c_m, z_s, z_m, gi_s, gi_m, gz_s, gz_m,
):
    dep = lax.axis_index("depth")
    row = lax.axis_index("row")
    y = lax.axis_index("col")
    zh, co = dep // 2, dep % 2
    x, zl = row // 2, row % 2
    yp, ym, yo = (y + 1) % 4, (y + 3) % 4, (y + 2) % 4
    up_dev = (dep, row, yp)
    dn_dev = (dep, row, ym)
    zhi_dep = (1 - zh) * 2 + co
    core_dep = zh * 2 + (1 - co)
    zhi_dev = (zhi_dep, row, y)
    core_dev = (core_dep, row, y)
    zlo_row = x * 2 + (1 - zl)
    zlo_dev = (dep, zlo_row, y)
    xs = [((x + d) % 4) * 2 + zl for d in (1, 3, 2)]
    x_dev = [(dep, r, y) for r in xs]

    def wait_recv(ref, sem, dev):
        remote(ref, ref, sem, sem, dev).wait_recv()

    def wait_send(ref, sem, dev):
        remote(ref, ref, sem, sem, dev).wait_send()

    def rows(r, n):
        return pl.ds(pl.multiple_of(r * n, n), n)

    l_go = pltpu.make_async_copy(go_in, go.at[rows(row, 128)], loc.at[0])
    l_dw = pltpu.make_async_copy(dw_in, dw.at[:, rows(dep, 256)], loc.at[1])
    l_tk = pltpu.make_async_copy(tok_in, pin.at[rows(row, 128)], loc.at[2])

    def l_gp(j):
        c = pl.ds(j * CH, CH)
        return (
            pltpu.make_async_copy(gp_in.at[:, c], gpu.at[j, y, 0], loc.at[4 + j]),
            pltpu.make_async_copy(up_in.at[:, c], gpu.at[j, y, 1], loc.at[11 + j]),
        )

    def l_wg(j):
        c = pl.ds(j * CH, CH)
        return (
            pltpu.make_async_copy(gw_in.at[:, c], wgu.at[j, rows(dep, 256), 0:CH], loc.at[18 + j]),
            pltpu.make_async_copy(
                uw_in.at[:, c], wgu.at[j, rows(dep, 256), CH : 2 * CH], loc.at[25 + j]
            ),
        )

    l_go.start()
    for c in l_gp(0):
        c.start()
    l_dw.start()
    for j in range(1, NC):
        for c in l_gp(j):
            c.start()
    for j in range(NC):
        for c in l_wg(j):
            c.start()
    l_tk.start()

    barrier = pltpu.get_barrier_semaphore()
    peers = [up_dev, dn_dev, zhi_dev, core_dev]
    for d in range(1, 8):
        peers.append((dep, (row + d) % 8, y))
    for dev in peers:
        pl.semaphore_signal(barrier, inc=1, device_id=dev, device_id_type=MESH)
    pl.semaphore_wait(barrier, len(peers))

    def row_sends(buf, ssem, rsem, r, which):
        ref = buf.at[rows(r, 128)]
        cps = [remote(ref, ref, ssem.at[which, i], rsem.at[r], x_dev[i]) for i in range(3)]
        if which == 0:
            cps.append(remote(ref, ref, ssem.at[0, 3], rsem.at[r], zlo_dev))
        return cps

    def dw_ref(p):
        return dw.at[:, rows(p, 256)]

    def wg_ref(j, p):
        return wgu.at[j, rows(p, 256)]

    def gp_step1(j):
        ref = gpu.at[j, y]
        return (
            remote(ref, ref, gp_s.at[j, 0], gp_r.at[j, 0], up_dev),
            remote(ref, ref, gp_s.at[j, 1], gp_r.at[j, 1], dn_dev),
        )

    def gp_step2(j):
        a, b = gpu.at[j, ym, 0], gpu.at[j, yp, 1]
        return (
            remote(a, a, gp_s.at[j, 2], gp_r.at[j, 2], up_dev),
            remote(b, b, gp_s.at[j, 3], gp_r.at[j, 3], dn_dev),
        )

    def gp_relay(j):
        f, s = gp_step2(j)
        wait_recv(gpu.at[j, ym], gp_r.at[j, 0], dn_dev)
        f.start()
        wait_recv(gpu.at[j, yp], gp_r.at[j, 1], up_dev)
        s.start()

    def wg_send(j):
        ref = wg_ref(j, dep)
        return (
            remote(ref, ref, wg_s.at[j, 0], wg_r.at[j, 0], zhi_dev),
            remote(ref, ref, wg_s.at[j, 1], wg_r.at[j, 1], core_dev),
        )

    def wg_fwd(j):
        ref = wg_ref(j, zhi_dep)
        return remote(ref, ref, wg_s.at[j, 2], wg_r.at[j, 2], core_dev)

    l_go.wait()
    for c in row_sends(go, go_s, go_r, row, 0):
        c.start()
    for c in l_gp(0):
        c.wait()
    for c in gp_step1(0):
        c.start()
    l_dw.wait()
    ref = dw_ref(dep)
    dw_a = remote(ref, ref, dw_s.at[0], dw_r.at[0], zhi_dev)
    dw_b = remote(ref, ref, dw_s.at[1], dw_r.at[1], core_dev)
    dw_a.start()
    dw_b.start()
    for j in range(1, NC):
        for c in l_gp(j):
            c.wait()
        if j < AHEAD:
            for c in gp_step1(j):
                c.start()
    wait_recv(go.at[rows(zlo_row, 128)], go_r.at[zlo_row], zlo_dev)
    for c in row_sends(go, go_s, go_r, zlo_row, 1):
        c.start()
    for j in range(NC):
        for c in l_wg(j):
            c.wait()
    l_tk.wait()
    acc[...] = jnp.zeros_like(acc)
    for j in range(AHEAD):
        gp_relay(j)
        if j == 1:
            for c in row_sends(pin, tk_s, tk_r, row, 0):
                c.start()
    wait_recv(dw_ref(zhi_dep), dw_r.at[0], zhi_dev)
    ref = dw_ref(zhi_dep)
    dw_c = remote(ref, ref, dw_s.at[2], dw_r.at[2], core_dev)
    dw_c.start()
    for j in range(NC):
        for c in wg_send(j):
            c.start()
    wait_recv(dw_ref(core_dep), dw_r.at[1], core_dev)
    for i in range(3):
        wait_recv(go.at[rows(xs[i], 128)], go_r.at[xs[i]], x_dev[i])
    for d in (1, 3, 2):
        r = ((x + d) % 4) * 2 + (1 - zl)
        wait_recv(go.at[rows(r, 128)], go_r.at[r], zlo_dev)
    wait_recv(dw_ref((1 - zh) * 2 + (1 - co)), dw_r.at[2], core_dev)

    def rs1_copies(k):
        return (
            remote(rs1s.at[k, 0:128], rs1r.at[k, 0], rs1_s.at[k, 0], rs1_m.at[k, 0], up_dev),
            remote(rs1s.at[k, 128:256], rs1r.at[k, 1], rs1_s.at[k, 1], rs1_m.at[k, 1], dn_dev),
        )

    def rs2_copies(k):
        return (
            remote(rs2s.at[k, 0], rs2r.at[k, 0], rs2_s.at[k, 0], rs2_m.at[k, 0], up_dev),
            remote(rs2s.at[k, 1], rs2r.at[k, 1], rs2_s.at[k, 1], rs2_m.at[k, 1], dn_dev),
        )

    def ag1_copies(k):
        ref = hid.at[k, y]
        return (
            remote(ref, ref, ag1_s.at[k, 0], ag1_m.at[k, 0], up_dev),
            remote(ref, ref, ag1_s.at[k, 1], ag1_m.at[k, 1], dn_dev),
        )

    def ag2_copies(k):
        a, b = hid.at[k, ym, 0:128], hid.at[k, yp, 128:256]
        return (
            remote(a, a, ag2_s.at[k, 0], ag2_m.at[k, 0], up_dev),
            remote(b, b, ag2_s.at[k, 1], ag2_m.at[k, 1], dn_dev),
        )

    def stage_a(k):
        w = dw[rows(k, CH), :]

        def part(q):
            return dot_nt(go[rows(q, 256), :], w)

        rs1s[k] = part(yo).astype(BF)
        for c in rs1_copies(k):
            c.start()
        nb[0] = part(yp)
        nb[1] = part(ym)
        own[k % 2] = part(y)

    def stage_b(k):
        wait_recv(rs1r.at[k, 0], rs1_m.at[k, 0], dn_dev)
        f, s = rs2_copies(k)
        rs2s[k, 0, 0:128] = (nb[0, 0:128] + rs1r[k, 0].astype(F32)).astype(BF)
        rs2s[k, 0, 128:256] = nb[0, 128:256].astype(BF)
        f.start()
        wait_recv(rs1r.at[k, 1], rs1_m.at[k, 1], up_dev)
        rs2s[k, 1, 0:128] = nb[1, 0:128].astype(BF)
        rs2s[k, 1, 128:256] = (nb[1, 128:256] + rs1r[k, 1].astype(F32)).astype(BF)
        s.start()

    def stage_c(k):
        wait_recv(rs2r.at[k, 0], rs2_m.at[k, 0], dn_dev)
        wait_recv(rs2r.at[k, 1], rs2_m.at[k, 1], up_dev)
        hid[k, y] = (own[k % 2] + rs2r[k, 0].astype(F32) + rs2r[k, 1].astype(F32)).astype(BF)
        for c in ag1_copies(k):
            c.start()

    def stage_d(k):
        f, s = ag2_copies(k)
        wait_recv(hid.at[k, ym], ag1_m.at[k, 0], dn_dev)
        f.start()
        wait_recv(hid.at[k, yp], ag1_m.at[k, 1], up_dev)
        s.start()

    def core_copy(j):
        return remote(cs.at[j % 2], cr.at[j], c_s.at[j], c_m.at[j], core_dev)

    def z_copy(j):
        return remote(zs.at[j % 2], zr.at[j], z_s.at[j], z_m.at[j], zhi_dev)

    def grad_parts(p):
        a = dot_nn(tkt[rows(p, 256), :], ggu[...])
        b = dot_nn(act[...], go[:, rows(p, 256)])
        return a, b

    def stage_e1(j):
        wait_recv(gpu.at[j, yo, 0], gp_r.at[j, 2], dn_dev)
        wait_recv(gpu.at[j, yo, 1], gp_r.at[j, 3], up_dev)
        wait_recv(hid.at[j, yo, 0:128], ag2_m.at[j, 0], dn_dev)
        wait_recv(hid.at[j, yo, 128:256], ag2_m.at[j, 1], up_dev)

        @pl.loop(0, 16)
        def _(i):
            c = i // 4
            r = pl.ds(pl.multiple_of((i % 4) * 64, 64), 64)
            o = pl.ds(pl.multiple_of(i * 64, 64), 64)
            h = hid[j, c, r, :].astype(F32)
            g = gpu[j, c, 0, r, :].astype(F32)
            u = gpu[j, c, 1, r, :].astype(F32)
            s = jax.nn.sigmoid(g)
            w = g * s
            ac[o, :] = (w * u).astype(BF)
            ggu[o, 0:CH] = (h * u * s * (1.0 + g * (1.0 - s))).astype(BF)
            ggu[o, CH : 2 * CH] = (h * w).astype(BF)

        @pl.when(j == NC - 1)
        def _():
            grad_in_last(j)

        for c in range(4):
            act[:, c * 256 : (c + 1) * 256] = ac[c * 256 : (c + 1) * 256, :].T

        @pl.when(j >= 2)
        def _():
            core_copy(j - 2).wait_send()

        @pl.loop(0, 2)
        def _(h):
            a, b = grad_parts(h * 2 + (1 - co))
            cs[j % 2, h, :, 0 : 2 * CH] = a.astype(BF)
            cs[j % 2, h, :, 2 * CH : 3 * CH] = b.astype(BF)

        core_copy(j).start()

        @pl.loop(0, 2)
        def _(h):
            a, b = grad_parts(h * 2 + co)
            opart[h, :, 0 : 2 * CH] = a
            opart[h, :, 2 * CH : 3 * CH] = b

    xp, xm, xo = (x + 1) % 4, (x + 3) % 4, (x + 2) % 4

    def half(q, t, n):
        return pl.ds(pl.multiple_of((q * 2 + t) * 128 + n * 64, 64), 64)

    def gi_copy(t, i):
        src, dst, dev = (
            (half(xo, t, 0), g1.at[t, 0], x_dev[0]),
            (half(xo, t, 1), g1.at[t, 1], x_dev[1]),
            (half(xp, t, 1), g2.at[t, 0, 1], x_dev[0]),
            (half(xm, t, 0), g2.at[t, 1, 0], x_dev[1]),
            (half(xp, t, 0), g2.at[t, 0, 0], x_dev[0]),
            (half(xm, t, 1), g2.at[t, 1, 1], x_dev[1]),
        )[i]
        return remote(pin.at[src], dst, gi_s.at[t, i], gi_m.at[t, i], dev)

    def gi_relay(t):
        gi_copy(t, 0).wait_recv()
        pin[half(xp, t, 0)] = (acc[half(xp, t, 0)] + g1[t, 0].astype(F32)).astype(BF)
        gi_copy(t, 4).start()
        gi_copy(t, 1).wait_recv()
        pin[half(xm, t, 1)] = (acc[half(xm, t, 1)] + g1[t, 1].astype(F32)).astype(BF)
        gi_copy(t, 5).start()

    def gi_sum(t):
        for i in (2, 3, 4, 5):
            gi_copy(t, i).wait_recv()
        o = rows(x * 2 + t, 128)
        first = g2[t, 0].astype(F32) + g2[t, 1].astype(F32)
        return acc[o, :] + first.reshape(128, 1024)

    gz_copy = remote(gs, gz, gz_s, gz_m, zlo_dev)

    def wait_weights(j):
        wait_recv(wg_ref(j, core_dep), wg_r.at[j, 1], core_dev)
        wait_recv(wg_ref(j, (1 - zh) * 2 + (1 - co)), wg_r.at[j, 2], core_dev)

    def stage_e2(j):
        wait_weights(j)

        @pl.loop(0, 4)
        def _(q):
            o = rows(q, 256)
            acc[o, :] += dot_nt(ggu[o, :], wgu[j])

    def grad_in_last(j):
        wait_weights(j)

        def part(q):
            o = rows(q, 256)
            t = acc[o, :] + dot_nt(ggu[o, :], wgu[j])
            acc[o, :] = t
            pin[o, :] = t.astype(BF)

        part(xo)
        for i in (0, 1):
            gi_copy(1 - zl, i).start()
        part(xp)
        gi_copy(1 - zl, 2).start()
        part(xm)
        gi_copy(1 - zl, 3).start()
        for i in (0, 1, 2, 3):
            gi_copy(zl, i).start()
        part(x)

    def stage_f(j):
        @pl.when(j >= 2)
        def _():
            z_copy(j - 2).wait_send()

        wait_recv(cr.at[j], c_m.at[j], core_dev)
        zs[j % 2] = (opart[1 - zh] + cr[j, 1 - zh].astype(F32)).astype(BF)
        z_copy(j).start()
        oq[j % 2] = opart[zh] + cr[j, zh].astype(F32)

    def stage_g(j):
        wait_recv(zr.at[j], z_m.at[j], zhi_dev)
        t = (oq[j % 2] + zr[j].astype(F32)) * scale
        c = rows(j, CH)
        ggw_out[:, c] = t[:, 0:CH].astype(BF)
        guw_out[:, c] = t[:, CH : 2 * CH].astype(BF)
        gdw_out[c, :] = t[:, 2 * CH : 3 * CH].astype(BF)

    def when(cond):
        return pl.when(cond)

    def body(k, carry):
        @when(k < NC)
        def _():
            stage_a(k)

        @when((k >= 1) & (k < NC + 1))
        def _():
            stage_c(k - 1)

        @when((k >= AHEAD) & (k < NC))
        def _():
            for c in gp_step1(k):
                c.start()

        @when((k >= 1) & (k < NC + 1))
        def _():
            wait_recv(wg_ref(k - 1, zhi_dep), wg_r.at[k - 1, 0], zhi_dev)
            wg_fwd(k - 1).start()

        @when(k == 0)
        def _():
            wait_recv(pin.at[rows(zlo_row, 128)], tk_r.at[zlo_row], zlo_dev)
            for c in row_sends(pin, tk_s, tk_r, zlo_row, 1):
                c.start()

        @when((k >= 3) & (k < NC + 3))
        def _():
            stage_f(k - 3)

        @when((k >= 2) & (k < NC + 2))
        def _():
            stage_e1(k - 2)

        @when(k < NC)
        def _():
            stage_b(k)

        @when((k >= 1) & (k < NC + 1))
        def _():
            stage_d(k - 1)

        @when((k >= AHEAD) & (k < NC))
        def _():
            gp_relay(k)

        @when(k == 1)
        def _():
            for i in range(3):
                wait_recv(pin.at[rows(xs[i], 128)], tk_r.at[xs[i]], x_dev[i])
            for d in (1, 3, 2):
                r = ((x + d) % 4) * 2 + (1 - zl)
                wait_recv(pin.at[rows(r, 128)], tk_r.at[r], zlo_dev)
            for c in row_sends(pin, tk_s, tk_r, row, 0) + row_sends(pin, tk_s, tk_r, zlo_row, 1):
                c.wait_send()

            @pl.loop(0, 4)
            def _(q):
                o = rows(q, 256)
                tkt[:, o] = pin[o, :].T

        @when((k >= 2) & (k < NC + 1))
        def _():
            stage_e2(k - 2)

        @when(k >= 4)
        def _():
            stage_g(k - 4)

        return carry

    lax.fori_loop(0, NC + 2, body, 0)
    gi_relay(1 - zl)
    stage_f(NC - 1)
    gi_relay(zl)
    stage_g(NC - 2)
    gs[...] = gi_sum(1 - zl).astype(BF)
    gz_copy.start()
    stage_g(NC - 1)
    total = gi_sum(zl)
    gz_copy.wait_recv()
    gin_out[...] = (total + gz[...].astype(F32)).astype(BF)

    for c in row_sends(go, go_s, go_r, row, 0) + row_sends(go, go_s, go_r, zlo_row, 1):
        c.wait_send()
    dw_a.wait_send()
    dw_b.wait_send()
    dw_c.wait_send()
    for t in range(2):
        for i in range(6):
            gi_copy(t, i).wait_send()
    gz_copy.wait_send()

    def drain(j, carry):
        for c in (*gp_step1(j), *gp_step2(j), *wg_send(j), wg_fwd(j), *rs1_copies(j)):
            c.wait_send()
        for c in (*rs2_copies(j), *ag1_copies(j), *ag2_copies(j)):
            c.wait_send()

        @pl.when(j >= NC - 2)
        def _():
            core_copy(j).wait_send()
            z_copy(j).wait_send()

        return carry

    lax.fori_loop(0, NC, drain, 0)


def copy_kernel(a0, a1, a2, a3, b0, b1, b2, b3, sem):
    pairs = ((a0, b0), (a1, b1), (a2, b2), (a3, b3))
    copies = [pltpu.make_async_copy(a, b, sem.at[i]) for i, (a, b) in enumerate(pairs)]
    for c in copies:
        c.start()
    for c in copies:
        c.wait()


def shards(tokens_in, grad_out, gate_pre, up_pre, gate_weight, up_weight, down_weight):
    scale = 1.0 / math.sqrt(4096.0)
    dma = pltpu.SemaphoreType.DMA
    vm = pltpu.VMEM
    hbm = pl.BlockSpec(memory_space=pl.ANY)
    vmem = pl.BlockSpec(memory_space=pltpu.VMEM)
    outs = pl.pallas_call(
        functools.partial(kernel, scale),
        out_shape=[
            jax.ShapeDtypeStruct((128, 1024), BF),
            jax.ShapeDtypeStruct((256, 1792), BF),
            jax.ShapeDtypeStruct((256, 1792), BF),
            jax.ShapeDtypeStruct((1792, 256), BF),
        ],
        in_specs=[hbm] * 7,
        out_specs=[vmem] * 4,
        scratch_shapes=[
            vm((1024, 1024), BF),
            vm((1024, 1024), BF),
            vm((1792, 1024), BF),
            vm((NC, 1024, 2 * CH), BF),
            vm((NC, 4, 2, 256, CH), BF),
            vm((NC, 256, CH), BF),
            vm((NC, 2, 128, CH), BF),
            vm((NC, 2, 256, CH), BF),
            vm((NC, 2, 256, CH), BF),
            vm((2, 256, CH), F32),
            vm((2, 256, CH), F32),
            vm((NC, 4, 256, CH), BF),
            vm((1024, 2 * CH), BF),
            vm((1024, CH), BF),
            vm((CH, 1024), BF),
            vm((1024, 1024), F32),
            vm((1024, 1024), BF),
            vm((2, 2, 64, 1024), BF),
            vm((2, 2, 2, 64, 1024), BF),
            vm((128, 1024), BF),
            vm((128, 1024), BF),
            vm((2, 2, 256, 3 * CH), BF),
            vm((NC, 2, 256, 3 * CH), BF),
            vm((2, 256, 3 * CH), F32),
            vm((2, 256, 3 * CH), BF),
            vm((NC, 256, 3 * CH), BF),
            vm((2, 256, 3 * CH), F32),
            dma((32,)),
            dma((2, 4)), dma((8,)),
            dma((2, 4)), dma((8,)),
            dma((3,)), dma((3,)),
            dma((NC, 3)), dma((NC, 3)),
            dma((NC, 4)), dma((NC, 4)),
            dma((NC, 2)), dma((NC, 2)),
            dma((NC, 2)), dma((NC, 2)),
            dma((NC, 2)), dma((NC, 2)),
            dma((NC, 2)), dma((NC, 2)),
            dma((NC,)), dma((NC,)),
            dma((NC,)), dma((NC,)),
            dma((2, 6)), dma((2, 6)),
            dma, dma,
        ],
        compiler_params=pltpu.CompilerParams(
            collective_id=0, has_side_effects=True, vmem_limit_bytes=62 * 2**20
        ),
        cost_estimate=pl.CostEstimate(
            flops=22_500_000_000, bytes_accessed=20_000_000, transcendentals=2_000_000
        ),
        name="swiglu_backward",
    )(tokens_in, grad_out, gate_pre, up_pre, gate_weight, up_weight, down_weight)
    return tuple(
        pl.pallas_call(
            copy_kernel,
            out_shape=[jax.ShapeDtypeStruct(o.shape, o.dtype) for o in outs],
            in_specs=[hbm] * 4,
            out_specs=[vmem] * 4,
            scratch_shapes=[dma((4,))],
            name="write_outputs",
        )(*outs)
    )


def solution(mesh):
    return jax.shard_map(
        shards,
        mesh=mesh,
        in_specs=(
            P(("depth", "row"), "col"),
            P(("depth", "row"), "col"),
            P(("depth", "col"), "row"),
            P(("depth", "col"), "row"),
            P(("col", "depth"), "row"),
            P(("col", "depth"), "row"),
            P("row", ("col", "depth")),
        ),
        out_specs=(
            P(("depth", "row"), "col"),
            P(("col", "depth"), "row"),
            P(("col", "depth"), "row"),
            P("row", ("col", "depth")),
        ),
        check_vma=False,
    )
```

```python
import functools
import math

import jax
import jax.numpy as jnp
from jax import lax
from jax.experimental import pallas as pl
from jax.experimental.pallas import tpu as pltpu
from jax.sharding import PartitionSpec as P

MESH = pl.DeviceIdType.MESH
BF = jnp.bfloat16
F32 = jnp.float32
NC = 7
CH = 256
AHEAD = 4


def dot_nt(a, b):
    return lax.dot_general(a, b, (((1,), (1,)), ((), ())), preferred_element_type=F32)


def dot_nn(a, b):
    return lax.dot_general(a, b, (((1,), (0,)), ((), ())), preferred_element_type=F32)


def sigmoid(g):
    return 0.5 * jnp.tanh(0.5 * g) + 0.5


def remote(src, dst, ssem, rsem, dev):
    return pltpu.make_async_remote_copy(
        src_ref=src, dst_ref=dst, send_sem=ssem, recv_sem=rsem, device_id=dev, device_id_type=MESH
    )


def kernel(
    scale,
    tok_in, go_in, gp_in, up_in, gw_in, uw_in, dw_in,
    gin_out, ggw_out, guw_out, gdw_out,
    go, tkt, dw, wgu, gpu, rs1s, rs1r, rs2s, rs2r, nb, own, hid, ggu, ac, act, acc, pin, g1, g2, gs, gz,
    cs, cr, opart, zs, zr, oq,
    loc, go_s, go_r, tk_s, tk_r, dw_s, dw_r, wg_s, wg_r, gp_s, gp_r,
    rs1_s, rs1_m, rs2_s, rs2_m, ag1_s, ag1_m, ag2_s, ag2_m, c_s, c_m, z_s, z_m, gi_s, gi_m, gz_s, gz_m,
):
    dep = lax.axis_index("depth")
    row = lax.axis_index("row")
    y = lax.axis_index("col")
    zh, co = dep // 2, dep % 2
    x, zl = row // 2, row % 2
    yp, ym, yo = (y + 1) % 4, (y + 3) % 4, (y + 2) % 4
    up_dev = (dep, row, yp)
    dn_dev = (dep, row, ym)
    zhi_dep = (1 - zh) * 2 + co
    core_dep = zh * 2 + (1 - co)
    zhi_dev = (zhi_dep, row, y)
    core_dev = (core_dep, row, y)
    zlo_row = x * 2 + (1 - zl)
    zlo_dev = (dep, zlo_row, y)
    xs = [((x + d) % 4) * 2 + zl for d in (1, 3, 2)]
    x_dev = [(dep, r, y) for r in xs]

    def wait_recv(ref, sem, dev):
        remote(ref, ref, sem, sem, dev).wait_recv()

    def wait_send(ref, sem, dev):
        remote(ref, ref, sem, sem, dev).wait_send()

    def rows(r, n):
        return pl.ds(pl.multiple_of(r * n, n), n)

    l_go = pltpu.make_async_copy(go_in, go.at[rows(row, 128)], loc.at[0])
    l_dw = pltpu.make_async_copy(dw_in, dw.at[:, rows(dep, 256)], loc.at[1])
    l_tk = pltpu.make_async_copy(tok_in, pin.at[rows(row, 128)], loc.at[2])

    def l_gp(j):
        c = pl.ds(j * CH, CH)
        return (
            pltpu.make_async_copy(gp_in.at[:, c], gpu.at[j, y, 0], loc.at[4 + j]),
            pltpu.make_async_copy(up_in.at[:, c], gpu.at[j, y, 1], loc.at[11 + j]),
        )

    def l_wg(j):
        c = pl.ds(j * CH, CH)
        return (
            pltpu.make_async_copy(gw_in.at[:, c], wgu.at[j, rows(dep, 256), 0:CH], loc.at[18 + j]),
            pltpu.make_async_copy(
                uw_in.at[:, c], wgu.at[j, rows(dep, 256), CH : 2 * CH], loc.at[25 + j]
            ),
        )

    l_go.start()
    for c in l_gp(0):
        c.start()
    l_dw.start()
    for j in range(1, NC):
        for c in l_gp(j):
            c.start()
    for j in range(NC):
        for c in l_wg(j):
            c.start()
    l_tk.start()

    barrier = pltpu.get_barrier_semaphore()
    peers = [up_dev, dn_dev, zhi_dev, core_dev]
    for d in range(1, 8):
        peers.append((dep, (row + d) % 8, y))
    for dev in peers:
        pl.semaphore_signal(barrier, inc=1, device_id=dev, device_id_type=MESH)
    pl.semaphore_wait(barrier, len(peers))

    def row_sends(buf, ssem, rsem, r, which):
        ref = buf.at[rows(r, 128)]
        cps = [remote(ref, ref, ssem.at[which, i], rsem.at[r], x_dev[i]) for i in range(3)]
        if which == 0:
            cps.append(remote(ref, ref, ssem.at[0, 3], rsem.at[r], zlo_dev))
        return cps

    def dw_ref(p):
        return dw.at[:, rows(p, 256)]

    def wg_ref(j, p):
        return wgu.at[j, rows(p, 256)]

    def gp_step1(j):
        ref = gpu.at[j, y]
        return (
            remote(ref, ref, gp_s.at[j, 0], gp_r.at[j, 0], up_dev),
            remote(ref, ref, gp_s.at[j, 1], gp_r.at[j, 1], dn_dev),
        )

    def gp_step2(j):
        a, b = gpu.at[j, ym, 0], gpu.at[j, yp, 1]
        return (
            remote(a, a, gp_s.at[j, 2], gp_r.at[j, 2], up_dev),
            remote(b, b, gp_s.at[j, 3], gp_r.at[j, 3], dn_dev),
        )

    def gp_relay(j):
        f, s = gp_step2(j)
        wait_recv(gpu.at[j, ym], gp_r.at[j, 0], dn_dev)
        f.start()
        wait_recv(gpu.at[j, yp], gp_r.at[j, 1], up_dev)
        s.start()

    def wg_send(j):
        ref = wg_ref(j, dep)
        return (
            remote(ref, ref, wg_s.at[j, 0], wg_r.at[j, 0], zhi_dev),
            remote(ref, ref, wg_s.at[j, 1], wg_r.at[j, 1], core_dev),
        )

    def wg_fwd(j):
        ref = wg_ref(j, zhi_dep)
        return remote(ref, ref, wg_s.at[j, 2], wg_r.at[j, 2], core_dev)

    l_go.wait()
    for c in row_sends(go, go_s, go_r, row, 0):
        c.start()
    for c in l_gp(0):
        c.wait()
    for c in gp_step1(0):
        c.start()
    l_dw.wait()
    ref = dw_ref(dep)
    dw_a = remote(ref, ref, dw_s.at[0], dw_r.at[0], zhi_dev)
    dw_b = remote(ref, ref, dw_s.at[1], dw_r.at[1], core_dev)
    dw_a.start()
    dw_b.start()
    for j in range(1, NC):
        for c in l_gp(j):
            c.wait()
        if j < AHEAD:
            for c in gp_step1(j):
                c.start()
    wait_recv(go.at[rows(zlo_row, 128)], go_r.at[zlo_row], zlo_dev)
    for c in row_sends(go, go_s, go_r, zlo_row, 1):
        c.start()
    for j in range(NC):
        for c in l_wg(j):
            c.wait()
    l_tk.wait()
    acc[...] = jnp.zeros_like(acc)
    for j in range(AHEAD):
        gp_relay(j)
        if j == 1:
            for c in row_sends(pin, tk_s, tk_r, row, 0):
                c.start()
    wait_recv(dw_ref(zhi_dep), dw_r.at[0], zhi_dev)
    ref = dw_ref(zhi_dep)
    dw_c = remote(ref, ref, dw_s.at[2], dw_r.at[2], core_dev)
    dw_c.start()
    for j in range(NC):
        for c in wg_send(j):
            c.start()
    wait_recv(dw_ref(core_dep), dw_r.at[1], core_dev)
    for i in range(3):
        wait_recv(go.at[rows(xs[i], 128)], go_r.at[xs[i]], x_dev[i])
    for d in (1, 3, 2):
        r = ((x + d) % 4) * 2 + (1 - zl)
        wait_recv(go.at[rows(r, 128)], go_r.at[r], zlo_dev)
    wait_recv(dw_ref((1 - zh) * 2 + (1 - co)), dw_r.at[2], core_dev)

    def rs1_copies(k):
        return (
            remote(rs1s.at[k, 0:128], rs1r.at[k, 0], rs1_s.at[k, 0], rs1_m.at[k, 0], up_dev),
            remote(rs1s.at[k, 128:256], rs1r.at[k, 1], rs1_s.at[k, 1], rs1_m.at[k, 1], dn_dev),
        )

    def rs2_copies(k):
        return (
            remote(rs2s.at[k, 0], rs2r.at[k, 0], rs2_s.at[k, 0], rs2_m.at[k, 0], up_dev),
            remote(rs2s.at[k, 1], rs2r.at[k, 1], rs2_s.at[k, 1], rs2_m.at[k, 1], dn_dev),
        )

    def ag1_copies(k):
        ref = hid.at[k, y]
        return (
            remote(ref, ref, ag1_s.at[k, 0], ag1_m.at[k, 0], up_dev),
            remote(ref, ref, ag1_s.at[k, 1], ag1_m.at[k, 1], dn_dev),
        )

    def ag2_copies(k):
        a, b = hid.at[k, ym, 0:128], hid.at[k, yp, 128:256]
        return (
            remote(a, a, ag2_s.at[k, 0], ag2_m.at[k, 0], up_dev),
            remote(b, b, ag2_s.at[k, 1], ag2_m.at[k, 1], dn_dev),
        )

    def stage_a(k):
        w = dw[rows(k, CH), :]

        def part(q):
            return dot_nt(go[rows(q, 256), :], w)

        rs1s[k] = part(yo).astype(BF)
        for c in rs1_copies(k):
            c.start()
        nb[0] = part(yp)
        nb[1] = part(ym)
        own[k % 2] = part(y)

    def stage_b(k):
        wait_recv(rs1r.at[k, 0], rs1_m.at[k, 0], dn_dev)
        f, s = rs2_copies(k)
        rs2s[k, 0, 0:128] = (nb[0, 0:128] + rs1r[k, 0].astype(F32)).astype(BF)
        rs2s[k, 0, 128:256] = nb[0, 128:256].astype(BF)
        f.start()
        wait_recv(rs1r.at[k, 1], rs1_m.at[k, 1], up_dev)
        rs2s[k, 1, 0:128] = nb[1, 0:128].astype(BF)
        rs2s[k, 1, 128:256] = (nb[1, 128:256] + rs1r[k, 1].astype(F32)).astype(BF)
        s.start()

    def stage_c(k):
        wait_recv(rs2r.at[k, 0], rs2_m.at[k, 0], dn_dev)
        wait_recv(rs2r.at[k, 1], rs2_m.at[k, 1], up_dev)
        hid[k, y] = (own[k % 2] + rs2r[k, 0].astype(F32) + rs2r[k, 1].astype(F32)).astype(BF)
        for c in ag1_copies(k):
            c.start()

    def stage_d(k):
        f, s = ag2_copies(k)
        wait_recv(hid.at[k, ym], ag1_m.at[k, 0], dn_dev)
        f.start()
        wait_recv(hid.at[k, yp], ag1_m.at[k, 1], up_dev)
        s.start()

    def core_copy(j):
        return remote(cs.at[j % 2], cr.at[j], c_s.at[j], c_m.at[j], core_dev)

    def z_copy(j):
        return remote(zs.at[j % 2], zr.at[j], z_s.at[j], z_m.at[j], zhi_dev)

    def grad_parts(p):
        a = dot_nn(tkt[rows(p, 256), :], ggu[...])
        b = dot_nn(act[...], go[:, rows(p, 256)])
        return a, b

    def stage_e1(j):
        wait_recv(gpu.at[j, yo, 0], gp_r.at[j, 2], dn_dev)
        wait_recv(gpu.at[j, yo, 1], gp_r.at[j, 3], up_dev)
        wait_recv(hid.at[j, yo, 0:128], ag2_m.at[j, 0], dn_dev)
        wait_recv(hid.at[j, yo, 128:256], ag2_m.at[j, 1], up_dev)

        @pl.loop(0, 16)
        def _(i):
            c = i // 4
            r = pl.ds(pl.multiple_of((i % 4) * 64, 64), 64)
            o = pl.ds(pl.multiple_of(i * 64, 64), 64)
            h = hid[j, c, r, :].astype(F32)
            g = gpu[j, c, 0, r, :].astype(F32)
            u = gpu[j, c, 1, r, :].astype(F32)
            s = sigmoid(g)
            w = g * s
            ac[o, :] = (w * u).astype(BF)
            ggu[o, 0:CH] = (h * u * (s + w * (1.0 - s))).astype(BF)
            ggu[o, CH : 2 * CH] = (h * w).astype(BF)

        @pl.when(j == NC - 1)
        def _():
            grad_in_last(j)

    def stage_e3(j):
        for c in range(4):
            act[:, c * 256 : (c + 1) * 256] = ac[c * 256 : (c + 1) * 256, :].T

        @pl.when(j >= 2)
        def _():
            core_copy(j - 2).wait_send()

        @pl.loop(0, 2)
        def _(h):
            a, b = grad_parts(h * 2 + (1 - co))
            cs[j % 2, h, :, 0 : 2 * CH] = a.astype(BF)
            cs[j % 2, h, :, 2 * CH : 3 * CH] = b.astype(BF)

        core_copy(j).start()

        @pl.loop(0, 2)
        def _(h):
            a, b = grad_parts(h * 2 + co)
            opart[h, :, 0 : 2 * CH] = a
            opart[h, :, 2 * CH : 3 * CH] = b

    xp, xm, xo = (x + 1) % 4, (x + 3) % 4, (x + 2) % 4

    def half(q, t, n):
        return pl.ds(pl.multiple_of((q * 2 + t) * 128 + n * 64, 64), 64)

    def gi_copy(t, i):
        src, dst, dev = (
            (half(xo, t, 0), g1.at[t, 0], x_dev[0]),
            (half(xo, t, 1), g1.at[t, 1], x_dev[1]),
            (half(xp, t, 1), g2.at[t, 0, 1], x_dev[0]),
            (half(xm, t, 0), g2.at[t, 1, 0], x_dev[1]),
            (half(xp, t, 0), g2.at[t, 0, 0], x_dev[0]),
            (half(xm, t, 1), g2.at[t, 1, 1], x_dev[1]),
        )[i]
        return remote(pin.at[src], dst, gi_s.at[t, i], gi_m.at[t, i], dev)

    def gi_relay(t):
        gi_copy(t, 0).wait_recv()
        pin[half(xp, t, 0)] = (acc[half(xp, t, 0)] + g1[t, 0].astype(F32)).astype(BF)
        gi_copy(t, 4).start()
        gi_copy(t, 1).wait_recv()
        pin[half(xm, t, 1)] = (acc[half(xm, t, 1)] + g1[t, 1].astype(F32)).astype(BF)
        gi_copy(t, 5).start()

    def gi_sum(t):
        for i in (2, 3, 4, 5):
            gi_copy(t, i).wait_recv()
        o = rows(x * 2 + t, 128)
        first = g2[t, 0].astype(F32) + g2[t, 1].astype(F32)
        return acc[o, :] + first.reshape(128, 1024)

    gz_copy = remote(gs, gz, gz_s, gz_m, zlo_dev)

    def wait_weights(j):
        wait_recv(wg_ref(j, core_dep), wg_r.at[j, 1], core_dev)
        wait_recv(wg_ref(j, (1 - zh) * 2 + (1 - co)), wg_r.at[j, 2], core_dev)

    def stage_e2(j):
        wait_weights(j)

        @pl.loop(0, 4)
        def _(q):
            o = rows(q, 256)
            acc[o, :] += dot_nt(ggu[o, :], wgu[j])

    def grad_in_last(j):
        wait_weights(j)

        def part(q):
            o = rows(q, 256)
            t = acc[o, :] + dot_nt(ggu[o, :], wgu[j])
            acc[o, :] = t
            pin[o, :] = t.astype(BF)

        part(xo)
        for i in (0, 1):
            gi_copy(1 - zl, i).start()
        part(xp)
        gi_copy(1 - zl, 2).start()
        part(xm)
        gi_copy(1 - zl, 3).start()
        for i in (0, 1, 2, 3):
            gi_copy(zl, i).start()
        part(x)

    def stage_f(j):
        @pl.when(j >= 2)
        def _():
            z_copy(j - 2).wait_send()

        wait_recv(cr.at[j], c_m.at[j], core_dev)
        zs[j % 2] = (opart[1 - zh] + cr[j, 1 - zh].astype(F32)).astype(BF)
        z_copy(j).start()
        oq[j % 2] = opart[zh] + cr[j, zh].astype(F32)

    def stage_g(j):
        wait_recv(zr.at[j], z_m.at[j], zhi_dev)
        t = (oq[j % 2] + zr[j].astype(F32)) * scale
        c = rows(j, CH)
        ggw_out[:, c] = t[:, 0:CH].astype(BF)
        guw_out[:, c] = t[:, CH : 2 * CH].astype(BF)
        gdw_out[c, :] = t[:, 2 * CH : 3 * CH].astype(BF)

    def when(cond):
        return pl.when(cond)

    def body(k, carry):
        @when(k < NC)
        def _():
            stage_a(k)

        @when((k >= 1) & (k < NC + 1))
        def _():
            stage_c(k - 1)

        @when((k >= AHEAD) & (k < NC))
        def _():
            for c in gp_step1(k):
                c.start()

        @when((k >= 1) & (k < NC + 1))
        def _():
            wait_recv(wg_ref(k - 1, zhi_dep), wg_r.at[k - 1, 0], zhi_dev)
            wg_fwd(k - 1).start()

        @when(k == 0)
        def _():
            wait_recv(pin.at[rows(zlo_row, 128)], tk_r.at[zlo_row], zlo_dev)
            for c in row_sends(pin, tk_s, tk_r, zlo_row, 1):
                c.start()

        @when((k >= 3) & (k < NC + 3))
        def _():
            stage_f(k - 3)

        @when((k >= 2) & (k < NC + 2))
        def _():
            stage_e1(k - 2)

        @when(k < NC)
        def _():
            stage_b(k)

        @when((k >= 2) & (k < NC + 2))
        def _():
            stage_e3(k - 2)

        @when((k >= 1) & (k < NC + 1))
        def _():
            stage_d(k - 1)

        @when((k >= AHEAD) & (k < NC))
        def _():
            gp_relay(k)

        @when(k == 1)
        def _():
            for i in range(3):
                wait_recv(pin.at[rows(xs[i], 128)], tk_r.at[xs[i]], x_dev[i])
            for d in (1, 3, 2):
                r = ((x + d) % 4) * 2 + (1 - zl)
                wait_recv(pin.at[rows(r, 128)], tk_r.at[r], zlo_dev)
            for c in row_sends(pin, tk_s, tk_r, row, 0) + row_sends(pin, tk_s, tk_r, zlo_row, 1):
                c.wait_send()

            @pl.loop(0, 4)
            def _(q):
                o = rows(q, 256)
                tkt[:, o] = pin[o, :].T

        @when((k >= 2) & (k < NC + 1))
        def _():
            stage_e2(k - 2)

        @when(k >= 4)
        def _():
            stage_g(k - 4)

        return carry

    lax.fori_loop(0, NC + 2, body, 0)
    gi_relay(1 - zl)
    stage_f(NC - 1)
    gi_relay(zl)
    stage_g(NC - 2)
    gs[...] = gi_sum(1 - zl).astype(BF)
    gz_copy.start()
    stage_g(NC - 1)
    total = gi_sum(zl)
    gz_copy.wait_recv()
    gin_out[...] = (total + gz[...].astype(F32)).astype(BF)

    for c in row_sends(go, go_s, go_r, row, 0) + row_sends(go, go_s, go_r, zlo_row, 1):
        c.wait_send()
    dw_a.wait_send()
    dw_b.wait_send()
    dw_c.wait_send()
    for t in range(2):
        for i in range(6):
            gi_copy(t, i).wait_send()
    gz_copy.wait_send()

    def drain(j, carry):
        for c in (*gp_step1(j), *gp_step2(j), *wg_send(j), wg_fwd(j), *rs1_copies(j)):
            c.wait_send()
        for c in (*rs2_copies(j), *ag1_copies(j), *ag2_copies(j)):
            c.wait_send()

        @pl.when(j >= NC - 2)
        def _():
            core_copy(j).wait_send()
            z_copy(j).wait_send()

        return carry

    lax.fori_loop(0, NC, drain, 0)


def copy_kernel(a0, a1, a2, a3, b0, b1, b2, b3, sem):
    pairs = ((a0, b0), (a1, b1), (a2, b2), (a3, b3))
    copies = [pltpu.make_async_copy(a, b, sem.at[i]) for i, (a, b) in enumerate(pairs)]
    for c in copies:
        c.start()
    for c in copies:
        c.wait()


def shards(tokens_in, grad_out, gate_pre, up_pre, gate_weight, up_weight, down_weight):
    scale = 1.0 / math.sqrt(4096.0)
    dma = pltpu.SemaphoreType.DMA
    vm = pltpu.VMEM
    hbm = pl.BlockSpec(memory_space=pl.ANY)
    vmem = pl.BlockSpec(memory_space=pltpu.VMEM)
    outs = pl.pallas_call(
        functools.partial(kernel, scale),
        out_shape=[
            jax.ShapeDtypeStruct((128, 1024), BF),
            jax.ShapeDtypeStruct((256, 1792), BF),
            jax.ShapeDtypeStruct((256, 1792), BF),
            jax.ShapeDtypeStruct((1792, 256), BF),
        ],
        in_specs=[hbm] * 7,
        out_specs=[vmem] * 4,
        scratch_shapes=[
            vm((1024, 1024), BF),
            vm((1024, 1024), BF),
            vm((1792, 1024), BF),
            vm((NC, 1024, 2 * CH), BF),
            vm((NC, 4, 2, 256, CH), BF),
            vm((NC, 256, CH), BF),
            vm((NC, 2, 128, CH), BF),
            vm((NC, 2, 256, CH), BF),
            vm((NC, 2, 256, CH), BF),
            vm((2, 256, CH), F32),
            vm((2, 256, CH), F32),
            vm((NC, 4, 256, CH), BF),
            vm((1024, 2 * CH), BF),
            vm((1024, CH), BF),
            vm((CH, 1024), BF),
            vm((1024, 1024), F32),
            vm((1024, 1024), BF),
            vm((2, 2, 64, 1024), BF),
            vm((2, 2, 2, 64, 1024), BF),
            vm((128, 1024), BF),
            vm((128, 1024), BF),
            vm((2, 2, 256, 3 * CH), BF),
            vm((NC, 2, 256, 3 * CH), BF),
            vm((2, 256, 3 * CH), F32),
            vm((2, 256, 3 * CH), BF),
            vm((NC, 256, 3 * CH), BF),
            vm((2, 256, 3 * CH), F32),
            dma((32,)),
            dma((2, 4)), dma((8,)),
            dma((2, 4)), dma((8,)),
            dma((3,)), dma((3,)),
            dma((NC, 3)), dma((NC, 3)),
            dma((NC, 4)), dma((NC, 4)),
            dma((NC, 2)), dma((NC, 2)),
            dma((NC, 2)), dma((NC, 2)),
            dma((NC, 2)), dma((NC, 2)),
            dma((NC, 2)), dma((NC, 2)),
            dma((NC,)), dma((NC,)),
            dma((NC,)), dma((NC,)),
            dma((2, 6)), dma((2, 6)),
            dma, dma,
        ],
        compiler_params=pltpu.CompilerParams(
            collective_id=0, has_side_effects=True, vmem_limit_bytes=62 * 2**20
        ),
        cost_estimate=pl.CostEstimate(
            flops=22_500_000_000, bytes_accessed=20_000_000, transcendentals=2_000_000
        ),
        name="swiglu_backward",
    )(tokens_in, grad_out, gate_pre, up_pre, gate_weight, up_weight, down_weight)
    return tuple(
        pl.pallas_call(
            copy_kernel,
            out_shape=[jax.ShapeDtypeStruct(o.shape, o.dtype) for o in outs],
            in_specs=[hbm] * 4,
            out_specs=[vmem] * 4,
            scratch_shapes=[dma((4,))],
            name="write_outputs",
        )(*outs)
    )


def solution(mesh):
    return jax.shard_map(
        shards,
        mesh=mesh,
        in_specs=(
            P(("depth", "row"), "col"),
            P(("depth", "row"), "col"),
            P(("depth", "col"), "row"),
            P(("depth", "col"), "row"),
            P(("col", "depth"), "row"),
            P(("col", "depth"), "row"),
            P("row", ("col", "depth")),
        ),
        out_specs=(
            P(("depth", "row"), "col"),
            P(("col", "depth"), "row"),
            P(("col", "depth"), "row"),
            P("row", ("col", "depth")),
        ),
        check_vma=False,
    )
```

```python
import functools
import math

import jax
import jax.numpy as jnp
from jax import lax
from jax.experimental import pallas as pl
from jax.experimental.pallas import tpu as pltpu
from jax.sharding import PartitionSpec as P

MESH = pl.DeviceIdType.MESH
BF = jnp.bfloat16
F32 = jnp.float32
NC = 7
CH = 256
AHEAD, PASSED = 4, 4
SEND_AT = {4: 2, 5: 4, 6: 5}
PASS_AT = {4: 3, 5: 5, 6: 6}


def dot_nt(a, b):
    return lax.dot_general(a, b, (((1,), (1,)), ((), ())), preferred_element_type=F32)


def dot_nn(a, b):
    return lax.dot_general(a, b, (((1,), (0,)), ((), ())), preferred_element_type=F32)


def sigmoid(g):
    return 0.5 * jnp.tanh(0.5 * g) + 0.5


def remote(src, dst, ssem, rsem, dev):
    return pltpu.make_async_remote_copy(
        src_ref=src, dst_ref=dst, send_sem=ssem, recv_sem=rsem, device_id=dev, device_id_type=MESH
    )


def kernel(
    scale,
    tok_in, go_in, gp_in, up_in, gw_in, uw_in, dw_in,
    gin_out, ggw_out, guw_out, gdw_out,
    gin_v, ggw_v, guw_v, gdw_v,
    go, tkt, dw, wgu, gpu, rs1s, rs1r, rs2s, rs2r, nb, own, hid, ggu, ac, got, acc, pin, g1, g2, gs, gz,
    cs, cr, opart, zs, zr, oq,
    loc, go_s, go_r, tk_s, tk_r, dw_s, dw_r, wg_s, wg_r, gp_s, gp_r,
    rs1_s, rs1_m, rs2_s, rs2_m, ag1_s, ag1_m, ag2_s, ag2_m, c_s, c_m, z_s, z_m, gi_s, gi_m, gz_s, gz_m, out_s,
):
    dep = lax.axis_index("depth")
    row = lax.axis_index("row")
    y = lax.axis_index("col")
    zh, co = dep // 2, dep % 2
    x, zl = row // 2, row % 2
    yp, ym, yo = (y + 1) % 4, (y + 3) % 4, (y + 2) % 4
    up_dev = (dep, row, yp)
    dn_dev = (dep, row, ym)
    zhi_dep = (1 - zh) * 2 + co
    core_dep = zh * 2 + (1 - co)
    zhi_dev = (zhi_dep, row, y)
    core_dev = (core_dep, row, y)
    zlo_row = x * 2 + (1 - zl)
    zlo_dev = (dep, zlo_row, y)
    xs = [((x + d) % 4) * 2 + zl for d in (1, 3, 2)]
    x_dev = [(dep, r, y) for r in xs]
    xp, xm, xo = (x + 1) % 4, (x + 3) % 4, (x + 2) % 4

    def wait_recv(ref, sem, dev):
        remote(ref, ref, sem, sem, dev).wait_recv()

    def wait_send(ref, sem, dev):
        remote(ref, ref, sem, sem, dev).wait_send()

    def rows(r, n):
        return pl.ds(pl.multiple_of(r * n, n), n)

    l_go = pltpu.make_async_copy(go_in, go.at[rows(row, 128)], loc.at[0])
    l_dw = pltpu.make_async_copy(dw_in, dw.at[:, rows(dep, 256)], loc.at[1])
    l_tk = pltpu.make_async_copy(tok_in, pin.at[rows(row, 128)], loc.at[2])

    def l_gp(j):
        c = pl.ds(j * CH, CH)
        return (
            pltpu.make_async_copy(gp_in.at[:, c], gpu.at[j, y, 0], loc.at[4 + j]),
            pltpu.make_async_copy(up_in.at[:, c], gpu.at[j, y, 1], loc.at[11 + j]),
        )

    def l_wg(j):
        c = pl.ds(j * CH, CH)
        return (
            pltpu.make_async_copy(gw_in.at[:, c], wgu.at[j, rows(dep, 256), 0:CH], loc.at[18 + j]),
            pltpu.make_async_copy(
                uw_in.at[:, c], wgu.at[j, rows(dep, 256), CH : 2 * CH], loc.at[25 + j]
            ),
        )

    l_go.start()
    for c in l_gp(0):
        c.start()
    l_dw.start()
    for j in range(1, NC):
        for c in l_gp(j):
            c.start()
    for j in range(NC):
        for c in l_wg(j):
            c.start()
    l_tk.start()

    barrier = pltpu.get_barrier_semaphore()
    peers = [up_dev, dn_dev, zhi_dev, core_dev]
    for d in range(1, 8):
        peers.append((dep, (row + d) % 8, y))
    for dev in peers:
        pl.semaphore_signal(barrier, inc=1, device_id=dev, device_id_type=MESH)
    pl.semaphore_wait(barrier, len(peers))

    def block(q, t):
        return pl.ds(pl.multiple_of((q * 2 + t) * 128, 128), 128)

    def half(q, t, n):
        return pl.ds(pl.multiple_of((q * 2 + t) * 128 + n * 64, 64), 64)

    zo = 1 - zl

    def row_copy(buf, sems, i):
        o, dev = (
            (block(x, zl), x_dev[0]),
            (block(x, zl), x_dev[1]),
            (block(x, zl), zlo_dev),
            (block(x, zo), x_dev[0]),
            (block(x, zo), x_dev[1]),
            (half(xm, zl, 0), x_dev[0]),
            (half(xp, zl, 1), x_dev[1]),
            (half(xm, zo, 0), x_dev[0]),
            (half(xp, zo, 1), x_dev[1]),
        )[i]
        return remote(buf.at[o], buf.at[o], sems[0].at[i], sems[1].at[i], dev)

    def row_start(buf, sems, *steps):
        for i in steps:
            row_copy(buf, sems, i).start()

    def row_wait(buf, sems, *steps):
        for i in steps:
            o = (
                block(xm, zl),
                block(xp, zl),
                block(x, zo),
                block(xm, zo),
                block(xp, zo),
                half(xo, zl, 0),
                half(xo, zl, 1),
                half(xo, zo, 0),
                half(xo, zo, 1),
            )[i]
            wait_recv(buf.at[o], sems[1].at[i], zlo_dev)

    def row_sent(buf, sems):
        for i in range(9):
            row_copy(buf, sems, i).wait_send()

    go_sem = (go_s, go_r)

    def row_sends(buf, ssem, rsem, r, which):
        ref = buf.at[rows(r, 128)]
        cps = [remote(ref, ref, ssem.at[which, i], rsem.at[r], x_dev[i]) for i in range(3)]
        if which == 0:
            cps.append(remote(ref, ref, ssem.at[0, 3], rsem.at[r], zlo_dev))
        return cps

    def dw_ref(p):
        return dw.at[:, rows(p, 256)]

    def wg_ref(j, p):
        return wgu.at[j, rows(p, 256)]

    def gp_step1(j):
        ref = gpu.at[j, y]
        return (
            remote(ref, ref, gp_s.at[j, 0], gp_r.at[j, 0], up_dev),
            remote(ref, ref, gp_s.at[j, 1], gp_r.at[j, 1], dn_dev),
        )

    def gp_step2(j):
        a, b = gpu.at[j, ym, 0], gpu.at[j, yp, 1]
        return (
            remote(a, a, gp_s.at[j, 2], gp_r.at[j, 2], up_dev),
            remote(b, b, gp_s.at[j, 3], gp_r.at[j, 3], dn_dev),
        )

    def gp_relay(j):
        f, s = gp_step2(j)
        wait_recv(gpu.at[j, ym], gp_r.at[j, 0], dn_dev)
        f.start()
        wait_recv(gpu.at[j, yp], gp_r.at[j, 1], up_dev)
        s.start()

    def wg_send(j):
        ref = wg_ref(j, dep)
        return (
            remote(ref, ref, wg_s.at[j, 0], wg_r.at[j, 0], zhi_dev),
            remote(ref, ref, wg_s.at[j, 1], wg_r.at[j, 1], core_dev),
        )

    def wg_fwd(j):
        ref = wg_ref(j, zhi_dep)
        return remote(ref, ref, wg_s.at[j, 2], wg_r.at[j, 2], core_dev)

    l_go.wait()
    row_start(go, go_sem, 2, 0, 1)
    for c in l_gp(0):
        c.wait()
    for c in gp_step1(0):
        c.start()
    l_dw.wait()
    ref = dw_ref(dep)
    dw_a = remote(ref, ref, dw_s.at[0], dw_r.at[0], zhi_dev)
    dw_b = remote(ref, ref, dw_s.at[1], dw_r.at[1], core_dev)
    dw_a.start()
    dw_b.start()
    for j in range(1, NC):
        for c in l_gp(j):
            c.wait()
        if j < AHEAD:
            for c in gp_step1(j):
                c.start()
    row_wait(go, go_sem, 2)
    row_start(go, go_sem, 3, 4)
    row_wait(go, go_sem, 0)
    row_start(go, go_sem, 5)
    row_wait(go, go_sem, 1)
    row_start(go, go_sem, 6)
    for j in range(NC):
        for c in l_wg(j):
            c.wait()
    l_tk.wait()
    acc[...] = jnp.zeros_like(acc)
    gp_relay(0)
    row_wait(go, go_sem, 3)
    row_start(go, go_sem, 7)
    row_wait(go, go_sem, 4)
    row_start(go, go_sem, 8)
    for c in row_sends(pin, tk_s, tk_r, row, 0):
        c.start()
    for j in range(1, PASSED):
        gp_relay(j)
    wait_recv(dw_ref(zhi_dep), dw_r.at[0], zhi_dev)
    ref = dw_ref(zhi_dep)
    dw_c = remote(ref, ref, dw_s.at[2], dw_r.at[2], core_dev)
    dw_c.start()
    for j in range(NC):
        for c in wg_send(j):
            c.start()
    wait_recv(dw_ref(core_dep), dw_r.at[1], core_dev)
    row_wait(go, go_sem, 5, 6, 7, 8)
    wait_recv(dw_ref((1 - zh) * 2 + (1 - co)), dw_r.at[2], core_dev)

    def rs1_copies(k):
        return (
            remote(rs1s.at[k, 0:128], rs1r.at[k, 0], rs1_s.at[k, 0], rs1_m.at[k, 0], up_dev),
            remote(rs1s.at[k, 128:256], rs1r.at[k, 1], rs1_s.at[k, 1], rs1_m.at[k, 1], dn_dev),
        )

    def rs2_copies(k):
        return (
            remote(rs2s.at[k, 0], rs2r.at[k, 0], rs2_s.at[k, 0], rs2_m.at[k, 0], up_dev),
            remote(rs2s.at[k, 1], rs2r.at[k, 1], rs2_s.at[k, 1], rs2_m.at[k, 1], dn_dev),
        )

    def ag1_copies(k):
        ref = hid.at[k, y]
        return (
            remote(ref, ref, ag1_s.at[k, 0], ag1_m.at[k, 0], up_dev),
            remote(ref, ref, ag1_s.at[k, 1], ag1_m.at[k, 1], dn_dev),
        )

    def ag2_copies(k):
        a, b = hid.at[k, ym, 0:128], hid.at[k, yp, 128:256]
        return (
            remote(a, a, ag2_s.at[k, 0], ag2_m.at[k, 0], up_dev),
            remote(b, b, ag2_s.at[k, 1], ag2_m.at[k, 1], dn_dev),
        )

    def stage_a(k):
        w = dw[rows(k, CH), :]

        def part(q):
            return dot_nt(go[rows(q, 256), :], w)

        rs1s[k] = part(yo).astype(BF)
        for c in rs1_copies(k):
            c.start()
        nb[0] = part(yp)
        nb[1] = part(ym)
        own[k % 2] = part(y)

    def stage_b(k):
        wait_recv(rs1r.at[k, 0], rs1_m.at[k, 0], dn_dev)
        f, s = rs2_copies(k)
        rs2s[k, 0, 0:128] = (nb[0, 0:128] + rs1r[k, 0].astype(F32)).astype(BF)
        rs2s[k, 0, 128:256] = nb[0, 128:256].astype(BF)
        f.start()
        wait_recv(rs1r.at[k, 1], rs1_m.at[k, 1], up_dev)
        rs2s[k, 1, 0:128] = nb[1, 0:128].astype(BF)
        rs2s[k, 1, 128:256] = (nb[1, 128:256] + rs1r[k, 1].astype(F32)).astype(BF)
        s.start()

    def stage_c(k):
        wait_recv(rs2r.at[k, 0], rs2_m.at[k, 0], dn_dev)
        wait_recv(rs2r.at[k, 1], rs2_m.at[k, 1], up_dev)
        hid[k, y] = (own[k % 2] + rs2r[k, 0].astype(F32) + rs2r[k, 1].astype(F32)).astype(BF)
        for c in ag1_copies(k):
            c.start()

    def stage_d(k):
        f, s = ag2_copies(k)
        wait_recv(hid.at[k, ym], ag1_m.at[k, 0], dn_dev)
        f.start()
        wait_recv(hid.at[k, yp], ag1_m.at[k, 1], up_dev)
        s.start()

    def core_copy(j):
        return remote(cs.at[j % 2], cr.at[j], c_s.at[j], c_m.at[j], core_dev)

    def z_copy(j):
        return remote(zs.at[j % 2], zr.at[j], z_s.at[j], z_m.at[j], zhi_dev)

    def grad_parts(c):
        a = dot_nn(tkt[:, c].reshape(512, 1024), ggu[...])
        b = dot_nn(got[:, c].reshape(512, 1024), ac[...])
        return a.reshape(2, 256, 2 * CH), b.reshape(2, 256, CH)

    def stage_e1(j):
        wait_recv(gpu.at[j, yo, 0], gp_r.at[j, 2], dn_dev)
        wait_recv(gpu.at[j, yo, 1], gp_r.at[j, 3], up_dev)
        wait_recv(hid.at[j, yo, 0:128], ag2_m.at[j, 0], dn_dev)
        wait_recv(hid.at[j, yo, 128:256], ag2_m.at[j, 1], up_dev)

        @pl.loop(0, 16)
        def _(i):
            c = i // 4
            r = pl.ds(pl.multiple_of((i % 4) * 64, 64), 64)
            o = pl.ds(pl.multiple_of(i * 64, 64), 64)
            h = hid[j, c, r, :].astype(F32)
            g = gpu[j, c, 0, r, :].astype(F32)
            u = gpu[j, c, 1, r, :].astype(F32)
            s = sigmoid(g)
            w = g * s
            ac[o, :] = (w * u).astype(BF)
            ggu[o, 0:CH] = (h * u * (s + w * (1.0 - s))).astype(BF)
            ggu[o, CH : 2 * CH] = (h * w).astype(BF)

        @pl.when(j == NC - 1)
        def _():
            grad_in_last(j)

    def stage_e3(j):
        @pl.when(j >= 2)
        def _():
            core_copy(j - 2).wait_send()

        a, b = grad_parts(1 - co)
        cs[j % 2, :, :, 0 : 2 * CH] = a.astype(BF)
        cs[j % 2, :, :, 2 * CH : 3 * CH] = b.astype(BF)
        core_copy(j).start()
        a, b = grad_parts(co)
        opart[:, :, 0 : 2 * CH] = a
        opart[:, :, 2 * CH : 3 * CH] = b

    def gi_copy(t, i):
        src, dst, dev = (
            (half(xo, t, 0), g1.at[t, 0], x_dev[0]),
            (half(xo, t, 1), g1.at[t, 1], x_dev[1]),
            (half(xp, t, 1), g2.at[t, 0, 1], x_dev[0]),
            (half(xm, t, 0), g2.at[t, 1, 0], x_dev[1]),
            (half(xp, t, 0), g2.at[t, 0, 0], x_dev[0]),
            (half(xm, t, 1), g2.at[t, 1, 1], x_dev[1]),
        )[i]
        return remote(pin.at[src], dst, gi_s.at[t, i], gi_m.at[t, i], dev)

    def gi_relay(t):
        gi_copy(t, 0).wait_recv()
        pin[half(xp, t, 0)] = (acc[half(xp, t, 0)] + g1[t, 0].astype(F32)).astype(BF)
        gi_copy(t, 4).start()
        gi_copy(t, 1).wait_recv()
        pin[half(xm, t, 1)] = (acc[half(xm, t, 1)] + g1[t, 1].astype(F32)).astype(BF)
        gi_copy(t, 5).start()

    def gi_sum(t):
        for i in (2, 3, 4, 5):
            gi_copy(t, i).wait_recv()
        o = rows(x * 2 + t, 128)
        first = g2[t, 0].astype(F32) + g2[t, 1].astype(F32)
        return acc[o, :] + first.reshape(128, 1024)

    gz_copy = remote(gs, gz, gz_s, gz_m, zlo_dev)

    def wait_weights(j):
        wait_recv(wg_ref(j, core_dep), wg_r.at[j, 1], core_dev)
        wait_recv(wg_ref(j, (1 - zh) * 2 + (1 - co)), wg_r.at[j, 2], core_dev)

    def stage_e2(j):
        wait_weights(j)

        @pl.loop(0, 4)
        def _(p):
            acc[:, rows(p, 256)] += dot_nt(ggu[...], wgu[j, rows(p, 256)])

    def grad_in_last(j):
        wait_weights(j)

        def part(q):
            o = rows(q, 256)
            t = acc[o, :] + dot_nt(ggu[o, :], wgu[j])
            acc[o, :] = t
            pin[o, :] = t.astype(BF)

        part(xo)
        for i in (0, 1):
            gi_copy(1 - zl, i).start()
        part(xp)
        gi_copy(1 - zl, 2).start()
        part(xm)
        gi_copy(1 - zl, 3).start()
        for i in (0, 1):
            gi_copy(zl, i).start()
        part(x)

    def stage_f(j):
        @pl.when(j >= 2)
        def _():
            z_copy(j - 2).wait_send()

        wait_recv(cr.at[j], c_m.at[j], core_dev)
        zs[j % 2] = (opart[1 - zh] + cr[j, 1 - zh].astype(F32)).astype(BF)
        z_copy(j).start()
        oq[j % 2] = opart[zh] + cr[j, zh].astype(F32)

    def out_copies(j):
        c = rows(j, CH)
        return (
            pltpu.make_async_copy(ggw_v.at[:, c], ggw_out.at[:, c], out_s.at[j, 0]),
            pltpu.make_async_copy(guw_v.at[:, c], guw_out.at[:, c], out_s.at[j, 1]),
            pltpu.make_async_copy(gdw_v.at[c], gdw_out.at[c], out_s.at[j, 2]),
        )

    def stage_g(j):
        wait_recv(zr.at[j], z_m.at[j], zhi_dev)
        t = (oq[j % 2] + zr[j].astype(F32)) * scale
        c = rows(j, CH)
        ggw_v[:, c] = t[:, 0:CH].astype(BF)
        guw_v[:, c] = t[:, CH : 2 * CH].astype(BF)
        gdw_v[c, :] = t[:, 2 * CH : 3 * CH].astype(BF).T
        for copy in out_copies(j):
            copy.start()

    def when(cond):
        return pl.when(cond)

    def body(k, carry):
        @when(k < NC)
        def _():
            stage_a(k)

        @when((k >= 1) & (k < NC + 1))
        def _():
            stage_c(k - 1)

        for j, step in SEND_AT.items():

            @when(k == step)
            def _():
                for c in gp_step1(j):
                    c.start()

        @when((k >= 1) & (k < NC + 1))
        def _():
            wait_recv(wg_ref(k - 1, zhi_dep), wg_r.at[k - 1, 0], zhi_dev)
            wg_fwd(k - 1).start()

        @when(k == 0)
        def _():
            wait_recv(pin.at[rows(zlo_row, 128)], tk_r.at[zlo_row], zlo_dev)
            for c in row_sends(pin, tk_s, tk_r, zlo_row, 1):
                c.start()

        @when((k >= 3) & (k < NC + 3))
        def _():
            stage_f(k - 3)

        @when((k >= 2) & (k < NC + 2))
        def _():
            stage_e1(k - 2)

        @when(k < NC)
        def _():
            stage_b(k)

        @when(k == 2)
        def _():
            for i in range(3):
                wait_recv(pin.at[rows(xs[i], 128)], tk_r.at[xs[i]], x_dev[i])
            for d in (1, 3, 2):
                r = ((x + d) % 4) * 2 + (1 - zl)
                wait_recv(pin.at[rows(r, 128)], tk_r.at[r], zlo_dev)
            for c in row_sends(pin, tk_s, tk_r, row, 0) + row_sends(pin, tk_s, tk_r, zlo_row, 1):
                c.wait_send()

            @pl.loop(0, 4)
            def _(q):
                o = rows(q, 256)
                tkt[:, :, :, o] = pin[o, :].T.reshape(2, 2, 256, 256)
                got[:, :, :, o] = go[o, :].T.reshape(2, 2, 256, 256)

        @when((k >= 2) & (k < NC + 2))
        def _():
            stage_e3(k - 2)

        @when((k >= 1) & (k < NC + 1))
        def _():
            stage_d(k - 1)

        for j, step in PASS_AT.items():

            @when(k == step)
            def _():
                gp_relay(j)

        @when((k >= 2) & (k < NC + 1))
        def _():
            stage_e2(k - 2)

        @when(k >= 4)
        def _():
            stage_g(k - 4)

        return carry

    lax.fori_loop(0, NC + 2, body, 0)
    gi_relay(1 - zl)
    for i in (2, 3):
        gi_copy(zl, i).start()
    stage_f(NC - 1)
    gi_relay(zl)
    stage_g(NC - 2)
    gs[...] = gi_sum(1 - zl).astype(BF)
    gz_copy.start()
    stage_g(NC - 1)
    total = gi_sum(zl)
    gz_copy.wait_recv()
    gin_v[...] = (total + gz[...].astype(F32)).astype(BF)
    gin_copy = pltpu.make_async_copy(gin_v, gin_out, loc.at[3])
    gin_copy.start()

    row_sent(go, go_sem)
    dw_a.wait_send()
    dw_b.wait_send()
    dw_c.wait_send()
    for t in range(2):
        for i in range(6):
            gi_copy(t, i).wait_send()
    gz_copy.wait_send()

    def drain(j, carry):
        for copy in out_copies(j):
            copy.wait()
        for c in (*gp_step1(j), *gp_step2(j), *wg_send(j), wg_fwd(j), *rs1_copies(j)):
            c.wait_send()
        for c in (*rs2_copies(j), *ag1_copies(j), *ag2_copies(j)):
            c.wait_send()

        @pl.when(j >= NC - 2)
        def _():
            core_copy(j).wait_send()
            z_copy(j).wait_send()

        return carry

    lax.fori_loop(0, NC, drain, 0)
    gin_copy.wait()


def copy_kernel(a0, a1, a2, a3, b0, b1, b2, b3, v0, v1, v2, v3, sem):
    sets = ((a0, v0, b0, 1), (a1, v1, b1, 4), (a2, v2, b2, 4), (a3, v3, b3, 4))
    pieces = []
    for a, v, b, n in sets:
        step = a.shape[0] // n
        pieces += [(a, v, b, pl.ds(i * step, step)) for i in range(n)]
    reads = [
        pltpu.make_async_copy(a.at[o], v.at[o], sem.at[0, i])
        for i, (a, v, _, o) in enumerate(pieces)
    ]
    writes = [
        pltpu.make_async_copy(v.at[o], b.at[o], sem.at[1, i])
        for i, (_, v, b, o) in enumerate(pieces)
    ]
    for c in reads:
        c.start()
    for r, w in zip(reads, writes):
        r.wait()
        w.start()
    for c in writes:
        c.wait()


def shards(tokens_in, grad_out, gate_pre, up_pre, gate_weight, up_weight, down_weight):
    scale = 1.0 / math.sqrt(4096.0)
    dma = pltpu.SemaphoreType.DMA
    vm = pltpu.VMEM
    hbm = pl.BlockSpec(memory_space=pl.ANY)
    vmem = pl.BlockSpec(memory_space=pltpu.VMEM)
    outs = pl.pallas_call(
        functools.partial(kernel, scale),
        out_shape=[
            jax.ShapeDtypeStruct((128, 1024), BF),
            jax.ShapeDtypeStruct((256, 1792), BF),
            jax.ShapeDtypeStruct((256, 1792), BF),
            jax.ShapeDtypeStruct((1792, 256), BF),
        ],
        in_specs=[hbm] * 7,
        out_specs=[hbm] * 4,
        scratch_shapes=[
            vm((128, 1024), BF),
            vm((256, 1792), BF),
            vm((256, 1792), BF),
            vm((1792, 256), BF),
            vm((1024, 1024), BF),
            vm((2, 2, 256, 1024), BF),
            vm((1792, 1024), BF),
            vm((NC, 1024, 2 * CH), BF),
            vm((NC, 4, 2, 256, CH), BF),
            vm((NC, 256, CH), BF),
            vm((NC, 2, 128, CH), BF),
            vm((NC, 2, 256, CH), BF),
            vm((NC, 2, 256, CH), BF),
            vm((2, 256, CH), F32),
            vm((2, 256, CH), F32),
            vm((NC, 4, 256, CH), BF),
            vm((1024, 2 * CH), BF),
            vm((1024, CH), BF),
            vm((2, 2, 256, 1024), BF),
            vm((1024, 1024), F32),
            vm((1024, 1024), BF),
            vm((2, 2, 64, 1024), BF),
            vm((2, 2, 2, 64, 1024), BF),
            vm((128, 1024), BF),
            vm((128, 1024), BF),
            vm((2, 2, 256, 3 * CH), BF),
            vm((NC, 2, 256, 3 * CH), BF),
            vm((2, 256, 3 * CH), F32),
            vm((2, 256, 3 * CH), BF),
            vm((NC, 256, 3 * CH), BF),
            vm((2, 256, 3 * CH), F32),
            dma((32,)),
            dma((9,)), dma((9,)),
            dma((2, 4)), dma((8,)),
            dma((3,)), dma((3,)),
            dma((NC, 3)), dma((NC, 3)),
            dma((NC, 4)), dma((NC, 4)),
            dma((NC, 2)), dma((NC, 2)),
            dma((NC, 2)), dma((NC, 2)),
            dma((NC, 2)), dma((NC, 2)),
            dma((NC, 2)), dma((NC, 2)),
            dma((NC,)), dma((NC,)),
            dma((NC,)), dma((NC,)),
            dma((2, 6)), dma((2, 6)),
            dma, dma,
            dma((NC, 3)),
        ],
        compiler_params=pltpu.CompilerParams(
            collective_id=0, has_side_effects=True, vmem_limit_bytes=62 * 2**20
        ),
        cost_estimate=pl.CostEstimate(
            flops=22_500_000_000, bytes_accessed=20_000_000, transcendentals=2_000_000
        ),
        name="swiglu_backward",
    )(tokens_in, grad_out, gate_pre, up_pre, gate_weight, up_weight, down_weight)
    return tuple(
        pl.pallas_call(
            copy_kernel,
            out_shape=[jax.ShapeDtypeStruct(o.shape, o.dtype) for o in outs],
            in_specs=[hbm] * 4,
            out_specs=[hbm] * 4,
            scratch_shapes=[*(vm(o.shape, o.dtype) for o in outs), dma((2, 13))],
            name="write_outputs",
        )(*outs)
    )


def solution(mesh):
    return jax.shard_map(
        shards,
        mesh=mesh,
        in_specs=(
            P(("depth", "row"), "col"),
            P(("depth", "row"), "col"),
            P(("depth", "col"), "row"),
            P(("depth", "col"), "row"),
            P(("col", "depth"), "row"),
            P(("col", "depth"), "row"),
            P("row", ("col", "depth")),
        ),
        out_specs=(
            P(("depth", "row"), "col"),
            P(("col", "depth"), "row"),
            P(("col", "depth"), "row"),
            P("row", ("col", "depth")),
        ),
        check_vma=False,
    )
```

```python
import functools
import math

import jax
import jax.numpy as jnp
from jax import lax
from jax.experimental import pallas as pl
from jax.experimental.pallas import tpu as pltpu
from jax.sharding import PartitionSpec as P

MESH = pl.DeviceIdType.MESH
BF = jnp.bfloat16
F32 = jnp.float32
NC = 7
CH = 256
AHEAD, PASSED = 4, 4
SEND_AT = {4: 2, 5: 4, 6: 5}
PASS_AT = {4: 3, 5: 5, 6: 6}


def dot_nt(a, b):
    return lax.dot_general(a, b, (((1,), (1,)), ((), ())), preferred_element_type=F32)


def dot_nn(a, b):
    return lax.dot_general(a, b, (((1,), (0,)), ((), ())), preferred_element_type=F32)


def sigmoid(g):
    return 0.5 * jnp.tanh(0.5 * g) + 0.5


def remote(src, dst, ssem, rsem, dev):
    return pltpu.make_async_remote_copy(
        src_ref=src, dst_ref=dst, send_sem=ssem, recv_sem=rsem, device_id=dev, device_id_type=MESH
    )


def kernel(
    scale,
    tok_in, go_in, gp_in, up_in, gw_in, uw_in, dw_in,
    gin_out, ggw_out, guw_out, gdw_out,
    gin_v, ggw_v, guw_v, gdw_v,
    go, tkt, dw, wgu, gpu, rs1s, rs1r, rs2s, rs2r, nb, own, hid, ggu, ac, got, acc, pin, g1, g2, gs, gz,
    cs, cr, opart, zs, zr, oq,
    loc, go_s, go_r, tk_s, tk_r, dw_s, dw_r, wg_s, wg_r, gp_s, gp_r,
    rs1_s, rs1_m, rs2_s, rs2_m, ag1_s, ag1_m, ag2_s, ag2_m, c_s, c_m, z_s, z_m, gi_s, gi_m, gz_s, gz_m, out_s,
):
    dep = lax.axis_index("depth")
    row = lax.axis_index("row")
    y = lax.axis_index("col")
    zh, co = dep // 2, dep % 2
    x, zl = row // 2, row % 2
    yp, ym, yo = (y + 1) % 4, (y + 3) % 4, (y + 2) % 4
    up_dev = (dep, row, yp)
    dn_dev = (dep, row, ym)
    zhi_dep = (1 - zh) * 2 + co
    core_dep = zh * 2 + (1 - co)
    zhi_dev = (zhi_dep, row, y)
    core_dev = (core_dep, row, y)
    zlo_row = x * 2 + (1 - zl)
    zlo_dev = (dep, zlo_row, y)
    xs = [((x + d) % 4) * 2 + zl for d in (1, 3, 2)]
    x_dev = [(dep, r, y) for r in xs]
    xp, xm, xo = (x + 1) % 4, (x + 3) % 4, (x + 2) % 4

    def wait_recv(ref, sem, dev):
        remote(ref, ref, sem, sem, dev).wait_recv()

    def wait_send(ref, sem, dev):
        remote(ref, ref, sem, sem, dev).wait_send()

    def rows(r, n):
        return pl.ds(pl.multiple_of(r * n, n), n)

    l_go = pltpu.make_async_copy(go_in, go.at[rows(row, 128)], loc.at[0])
    l_dw = pltpu.make_async_copy(dw_in, dw.at[:, rows(dep, 256)], loc.at[1])
    l_tk = pltpu.make_async_copy(tok_in, pin.at[rows(row, 128)], loc.at[2])

    def l_gp(j):
        c = pl.ds(j * CH, CH)
        return (
            pltpu.make_async_copy(gp_in.at[:, c], gpu.at[j, y, 0], loc.at[4 + j]),
            pltpu.make_async_copy(up_in.at[:, c], gpu.at[j, y, 1], loc.at[11 + j]),
        )

    def l_wg(j):
        c = pl.ds(j * CH, CH)
        return (
            pltpu.make_async_copy(gw_in.at[:, c], wgu.at[j, rows(dep, 256), 0:CH], loc.at[18 + j]),
            pltpu.make_async_copy(
                uw_in.at[:, c], wgu.at[j, rows(dep, 256), CH : 2 * CH], loc.at[25 + j]
            ),
        )

    for c in l_gp(0):
        c.start()
    l_go.start()
    l_dw.start()
    for j in range(1, NC):
        for c in l_gp(j):
            c.start()
    for j in range(NC):
        for c in l_wg(j):
            c.start()
    l_tk.start()

    barrier = pltpu.get_barrier_semaphore()
    peers = [up_dev, dn_dev, zhi_dev, core_dev]
    for d in range(1, 8):
        peers.append((dep, (row + d) % 8, y))
    for dev in peers:
        pl.semaphore_signal(barrier, inc=1, device_id=dev, device_id_type=MESH)
    pl.semaphore_wait(barrier, len(peers))

    def block(q, t):
        return pl.ds(pl.multiple_of((q * 2 + t) * 128, 128), 128)

    def half(q, t, n):
        return pl.ds(pl.multiple_of((q * 2 + t) * 128 + n * 64, 64), 64)

    zo = 1 - zl

    def row_copy(buf, sems, i):
        o, dev = (
            (block(x, zl), x_dev[0]),
            (block(x, zl), x_dev[1]),
            (block(x, zl), zlo_dev),
            (block(x, zo), x_dev[0]),
            (block(x, zo), x_dev[1]),
            (half(xm, zl, 0), x_dev[0]),
            (half(xp, zl, 1), x_dev[1]),
            (half(xm, zo, 0), x_dev[0]),
            (half(xp, zo, 1), x_dev[1]),
        )[i]
        return remote(buf.at[o], buf.at[o], sems[0].at[i], sems[1].at[i], dev)

    def row_start(buf, sems, *steps):
        for i in steps:
            row_copy(buf, sems, i).start()

    def row_wait(buf, sems, *steps):
        for i in steps:
            o = (
                block(xm, zl),
                block(xp, zl),
                block(x, zo),
                block(xm, zo),
                block(xp, zo),
                half(xo, zl, 0),
                half(xo, zl, 1),
                half(xo, zo, 0),
                half(xo, zo, 1),
            )[i]
            wait_recv(buf.at[o], sems[1].at[i], zlo_dev)

    def row_sent(buf, sems):
        for i in range(9):
            row_copy(buf, sems, i).wait_send()

    go_sem = (go_s, go_r)

    def row_sends(buf, ssem, rsem, r, which):
        ref = buf.at[rows(r, 128)]
        cps = [remote(ref, ref, ssem.at[which, i], rsem.at[r], x_dev[i]) for i in range(3)]
        if which == 0:
            cps.append(remote(ref, ref, ssem.at[0, 3], rsem.at[r], zlo_dev))
        return cps

    def dw_ref(p):
        return dw.at[:, rows(p, 256)]

    def wg_ref(j, p):
        return wgu.at[j, rows(p, 256)]

    def gp_step1(j):
        ref = gpu.at[j, y]
        return (
            remote(ref, ref, gp_s.at[j, 0], gp_r.at[j, 0], up_dev),
            remote(ref, ref, gp_s.at[j, 1], gp_r.at[j, 1], dn_dev),
        )

    def gp_step2(j):
        a, b = gpu.at[j, ym, 0], gpu.at[j, yp, 1]
        return (
            remote(a, a, gp_s.at[j, 2], gp_r.at[j, 2], up_dev),
            remote(b, b, gp_s.at[j, 3], gp_r.at[j, 3], dn_dev),
        )

    def gp_relay(j):
        f, s = gp_step2(j)
        wait_recv(gpu.at[j, ym], gp_r.at[j, 0], dn_dev)
        f.start()
        wait_recv(gpu.at[j, yp], gp_r.at[j, 1], up_dev)
        s.start()

    def wg_send(j):
        ref = wg_ref(j, dep)
        return (
            remote(ref, ref, wg_s.at[j, 0], wg_r.at[j, 0], zhi_dev),
            remote(ref, ref, wg_s.at[j, 1], wg_r.at[j, 1], core_dev),
        )

    def wg_fwd(j):
        ref = wg_ref(j, zhi_dep)
        return remote(ref, ref, wg_s.at[j, 2], wg_r.at[j, 2], core_dev)

    for c in l_gp(0):
        c.wait()
    for c in gp_step1(0):
        c.start()
    l_go.wait()
    row_start(go, go_sem, 2, 0, 1)
    l_dw.wait()
    ref = dw_ref(dep)
    dw_a = remote(ref, ref, dw_s.at[0], dw_r.at[0], zhi_dev)
    dw_b = remote(ref, ref, dw_s.at[1], dw_r.at[1], core_dev)
    dw_a.start()
    dw_b.start()
    for j in range(1, NC):
        for c in l_gp(j):
            c.wait()
        if j < AHEAD:
            for c in gp_step1(j):
                c.start()
    row_wait(go, go_sem, 2)
    row_start(go, go_sem, 3, 4)
    row_wait(go, go_sem, 0)
    row_start(go, go_sem, 5)
    row_wait(go, go_sem, 1)
    row_start(go, go_sem, 6)
    for j in range(NC):
        for c in l_wg(j):
            c.wait()
    l_tk.wait()
    gp_relay(0)
    row_wait(go, go_sem, 3)
    row_start(go, go_sem, 7)
    row_wait(go, go_sem, 4)
    row_start(go, go_sem, 8)
    for c in row_sends(pin, tk_s, tk_r, row, 0):
        c.start()
    for j in range(1, PASSED):
        gp_relay(j)
    wait_recv(dw_ref(zhi_dep), dw_r.at[0], zhi_dev)
    ref = dw_ref(zhi_dep)
    dw_c = remote(ref, ref, dw_s.at[2], dw_r.at[2], core_dev)
    dw_c.start()
    for j in range(NC):
        for c in wg_send(j):
            c.start()
    wait_recv(dw_ref(core_dep), dw_r.at[1], core_dev)
    row_wait(go, go_sem, 5, 6, 7, 8)
    wait_recv(dw_ref((1 - zh) * 2 + (1 - co)), dw_r.at[2], core_dev)

    def rs1_copies(k):
        return (
            remote(rs1s.at[k, 0:128], rs1r.at[k, 0], rs1_s.at[k, 0], rs1_m.at[k, 0], up_dev),
            remote(rs1s.at[k, 128:256], rs1r.at[k, 1], rs1_s.at[k, 1], rs1_m.at[k, 1], dn_dev),
        )

    def rs2_copies(k):
        return (
            remote(rs2s.at[k, 0], rs2r.at[k, 0], rs2_s.at[k, 0], rs2_m.at[k, 0], up_dev),
            remote(rs2s.at[k, 1], rs2r.at[k, 1], rs2_s.at[k, 1], rs2_m.at[k, 1], dn_dev),
        )

    def ag1_copies(k):
        ref = hid.at[k, y]
        return (
            remote(ref, ref, ag1_s.at[k, 0], ag1_m.at[k, 0], up_dev),
            remote(ref, ref, ag1_s.at[k, 1], ag1_m.at[k, 1], dn_dev),
        )

    def ag2_copies(k):
        a, b = hid.at[k, ym, 0:128], hid.at[k, yp, 128:256]
        return (
            remote(a, a, ag2_s.at[k, 0], ag2_m.at[k, 0], up_dev),
            remote(b, b, ag2_s.at[k, 1], ag2_m.at[k, 1], dn_dev),
        )

    def stage_a(k):
        w = dw[rows(k, CH), :]

        def part(q):
            return dot_nt(go[rows(q, 256), :], w)

        rs1s[k] = part(yo).astype(BF)
        for c in rs1_copies(k):
            c.start()
        nb[0] = part(yp)
        nb[1] = part(ym)
        own[k % 2] = part(y)

    def stage_b(k):
        wait_recv(rs1r.at[k, 0], rs1_m.at[k, 0], dn_dev)
        f, s = rs2_copies(k)
        rs2s[k, 0, 0:128] = (nb[0, 0:128] + rs1r[k, 0].astype(F32)).astype(BF)
        rs2s[k, 0, 128:256] = nb[0, 128:256].astype(BF)
        f.start()
        wait_recv(rs1r.at[k, 1], rs1_m.at[k, 1], up_dev)
        rs2s[k, 1, 0:128] = nb[1, 0:128].astype(BF)
        rs2s[k, 1, 128:256] = (nb[1, 128:256] + rs1r[k, 1].astype(F32)).astype(BF)
        s.start()

    def stage_c(k):
        wait_recv(rs2r.at[k, 0], rs2_m.at[k, 0], dn_dev)
        wait_recv(rs2r.at[k, 1], rs2_m.at[k, 1], up_dev)
        hid[k, y] = (own[k % 2] + rs2r[k, 0].astype(F32) + rs2r[k, 1].astype(F32)).astype(BF)
        for c in ag1_copies(k):
            c.start()

    def stage_d(k):
        f, s = ag2_copies(k)
        wait_recv(hid.at[k, ym], ag1_m.at[k, 0], dn_dev)
        f.start()
        wait_recv(hid.at[k, yp], ag1_m.at[k, 1], up_dev)
        s.start()

    def core_copy(j):
        return remote(cs.at[j % 2], cr.at[j], c_s.at[j], c_m.at[j], core_dev)

    def z_copy(j):
        return remote(zs.at[j % 2], zr.at[j], z_s.at[j], z_m.at[j], zhi_dev)

    def grad_parts(c):
        a = dot_nn(tkt[:, c].reshape(512, 1024), ggu[...])
        b = dot_nn(got[:, c].reshape(512, 1024), ac[...])
        return a.reshape(2, 256, 2 * CH), b.reshape(2, 256, CH)

    def stage_e1(j):
        wait_recv(gpu.at[j, yo, 0], gp_r.at[j, 2], dn_dev)
        wait_recv(gpu.at[j, yo, 1], gp_r.at[j, 3], up_dev)
        wait_recv(hid.at[j, yo, 0:128], ag2_m.at[j, 0], dn_dev)
        wait_recv(hid.at[j, yo, 128:256], ag2_m.at[j, 1], up_dev)

        @pl.loop(0, 16)
        def _(i):
            c = i // 4
            r = pl.ds(pl.multiple_of((i % 4) * 64, 64), 64)
            o = pl.ds(pl.multiple_of(i * 64, 64), 64)
            h = hid[j, c, r, :].astype(F32)
            g = gpu[j, c, 0, r, :].astype(F32)
            u = gpu[j, c, 1, r, :].astype(F32)
            s = sigmoid(g)
            w = g * s
            ac[o, :] = (w * u).astype(BF)
            ggu[o, 0:CH] = (h * u * (s + w * (1.0 - s))).astype(BF)
            ggu[o, CH : 2 * CH] = (h * w).astype(BF)

        @pl.when(j == NC - 1)
        def _():
            grad_in_last(j)

    def stage_e3(j):
        @pl.when(j >= 2)
        def _():
            core_copy(j - 2).wait_send()

        a, b = grad_parts(1 - co)
        cs[j % 2, :, :, 0 : 2 * CH] = a.astype(BF)
        cs[j % 2, :, :, 2 * CH : 3 * CH] = b.astype(BF)
        core_copy(j).start()
        a, b = grad_parts(co)
        opart[:, :, 0 : 2 * CH] = a
        opart[:, :, 2 * CH : 3 * CH] = b

    def gi_copy(t, i):
        src, dst, dev = (
            (half(xo, t, 0), g1.at[t, 0], x_dev[0]),
            (half(xo, t, 1), g1.at[t, 1], x_dev[1]),
            (half(xp, t, 1), g2.at[t, 0, 1], x_dev[0]),
            (half(xm, t, 0), g2.at[t, 1, 0], x_dev[1]),
            (half(xp, t, 0), g2.at[t, 0, 0], x_dev[0]),
            (half(xm, t, 1), g2.at[t, 1, 1], x_dev[1]),
        )[i]
        return remote(pin.at[src], dst, gi_s.at[t, i], gi_m.at[t, i], dev)

    def gi_relay(t):
        gi_copy(t, 0).wait_recv()
        pin[half(xp, t, 0)] = (acc[half(xp, t, 0)] + g1[t, 0].astype(F32)).astype(BF)
        gi_copy(t, 4).start()
        gi_copy(t, 1).wait_recv()
        pin[half(xm, t, 1)] = (acc[half(xm, t, 1)] + g1[t, 1].astype(F32)).astype(BF)
        gi_copy(t, 5).start()

    def gi_sum(t):
        for i in (2, 3, 4, 5):
            gi_copy(t, i).wait_recv()
        o = rows(x * 2 + t, 128)
        first = g2[t, 0].astype(F32) + g2[t, 1].astype(F32)
        return acc[o, :] + first.reshape(128, 1024)

    gz_copy = remote(gs, gz, gz_s, gz_m, zlo_dev)

    def wait_weights(j):
        wait_recv(wg_ref(j, core_dep), wg_r.at[j, 1], core_dev)
        wait_recv(wg_ref(j, (1 - zh) * 2 + (1 - co)), wg_r.at[j, 2], core_dev)

    def stage_e2(j):
        wait_weights(j)

        @pl.when(j == 0)
        def _():
            @pl.loop(0, 4)
            def _(p):
                acc[:, rows(p, 256)] = dot_nt(ggu[...], wgu[j, rows(p, 256)])

        @pl.when(j > 0)
        def _():
            @pl.loop(0, 4)
            def _(p):
                acc[:, rows(p, 256)] += dot_nt(ggu[...], wgu[j, rows(p, 256)])

    def grad_in_last(j):
        wait_weights(j)

        def part(q):
            o = rows(q, 256)
            t = acc[o, :] + dot_nt(ggu[o, :], wgu[j])
            acc[o, :] = t
            pin[o, :] = t.astype(BF)

        part(xo)
        for i in (0, 1):
            gi_copy(1 - zl, i).start()
        part(xp)
        gi_copy(1 - zl, 2).start()
        part(xm)
        gi_copy(1 - zl, 3).start()
        for i in (0, 1):
            gi_copy(zl, i).start()
        part(x)

    def stage_f(j):
        @pl.when(j >= 2)
        def _():
            z_copy(j - 2).wait_send()

        wait_recv(cr.at[j], c_m.at[j], core_dev)
        zs[j % 2] = (opart[1 - zh] + cr[j, 1 - zh].astype(F32)).astype(BF)
        z_copy(j).start()
        oq[j % 2] = opart[zh] + cr[j, zh].astype(F32)

    def out_copies(j):
        c = rows(j, CH)
        return (
            pltpu.make_async_copy(ggw_v.at[:, c], ggw_out.at[:, c], out_s.at[j, 0]),
            pltpu.make_async_copy(guw_v.at[:, c], guw_out.at[:, c], out_s.at[j, 1]),
            pltpu.make_async_copy(gdw_v.at[c], gdw_out.at[c], out_s.at[j, 2]),
        )

    def stage_g(j):
        wait_recv(zr.at[j], z_m.at[j], zhi_dev)
        t = (oq[j % 2] + zr[j].astype(F32)) * scale
        c = rows(j, CH)
        ggw_v[:, c] = t[:, 0:CH].astype(BF)
        guw_v[:, c] = t[:, CH : 2 * CH].astype(BF)
        gdw_v[c, :] = t[:, 2 * CH : 3 * CH].astype(BF).T
        for copy in out_copies(j):
            copy.start()

    def when(cond):
        return pl.when(cond)

    def body(k, carry):
        @when(k < NC)
        def _():
            stage_a(k)

        @when((k >= 1) & (k < NC + 1))
        def _():
            stage_c(k - 1)

        for j, step in SEND_AT.items():

            @when(k == step)
            def _():
                for c in gp_step1(j):
                    c.start()

        @when((k >= 1) & (k < NC + 1))
        def _():
            wait_recv(wg_ref(k - 1, zhi_dep), wg_r.at[k - 1, 0], zhi_dev)
            wg_fwd(k - 1).start()

        @when(k == 0)
        def _():
            wait_recv(pin.at[rows(zlo_row, 128)], tk_r.at[zlo_row], zlo_dev)
            for c in row_sends(pin, tk_s, tk_r, zlo_row, 1):
                c.start()

        @when((k >= 2) & (k < NC + 2))
        def _():
            stage_e1(k - 2)

        @when(k < NC)
        def _():
            stage_b(k)

        @when(k == 2)
        def _():
            for i in range(3):
                wait_recv(pin.at[rows(xs[i], 128)], tk_r.at[xs[i]], x_dev[i])
            for d in (1, 3, 2):
                r = ((x + d) % 4) * 2 + (1 - zl)
                wait_recv(pin.at[rows(r, 128)], tk_r.at[r], zlo_dev)
            for c in row_sends(pin, tk_s, tk_r, row, 0) + row_sends(pin, tk_s, tk_r, zlo_row, 1):
                c.wait_send()

            @pl.loop(0, 4)
            def _(q):
                o = rows(q, 256)
                tkt[:, :, :, o] = pin[o, :].T.reshape(2, 2, 256, 256)
                got[:, :, :, o] = go[o, :].T.reshape(2, 2, 256, 256)

        @when((k >= 2) & (k < NC + 2))
        def _():
            stage_e3(k - 2)

        @when((k >= 1) & (k < NC + 1))
        def _():
            stage_d(k - 1)

        for j, step in PASS_AT.items():

            @when(k == step)
            def _():
                gp_relay(j)

        @when((k >= 2) & (k < NC + 1))
        def _():
            stage_e2(k - 2)

        @when(k >= 4)
        def _():
            stage_g(k - 4)

        @when((k >= 2) & (k < NC + 1))
        def _():
            stage_f(k - 2)

        return carry

    lax.fori_loop(0, NC + 2, body, 0)
    gi_relay(1 - zl)
    for i in (2, 3):
        gi_copy(zl, i).start()
    gi_relay(zl)
    stage_f(NC - 1)
    stage_g(NC - 2)
    gs[...] = gi_sum(1 - zl).astype(BF)
    gz_copy.start()
    stage_g(NC - 1)
    total = gi_sum(zl)
    gz_copy.wait_recv()
    gin_v[...] = (total + gz[...].astype(F32)).astype(BF)
    gin_copy = pltpu.make_async_copy(gin_v, gin_out, loc.at[3])
    gin_copy.start()

    row_sent(go, go_sem)
    dw_a.wait_send()
    dw_b.wait_send()
    dw_c.wait_send()
    for t in range(2):
        for i in range(6):
            gi_copy(t, i).wait_send()
    gz_copy.wait_send()

    def drain(j, carry):
        for copy in out_copies(j):
            copy.wait()
        for c in (*gp_step1(j), *gp_step2(j), *wg_send(j), wg_fwd(j), *rs1_copies(j)):
            c.wait_send()
        for c in (*rs2_copies(j), *ag1_copies(j), *ag2_copies(j)):
            c.wait_send()

        @pl.when(j >= NC - 2)
        def _():
            core_copy(j).wait_send()
            z_copy(j).wait_send()

        return carry

    lax.fori_loop(0, NC, drain, 0)
    gin_copy.wait()


def copy_kernel(a0, a1, a2, a3, b0, b1, b2, b3, v0, v1, v2, v3, sem):
    sets = ((a0, v0, b0, 1), (a1, v1, b1, 4), (a2, v2, b2, 4), (a3, v3, b3, 4))
    pieces = []
    for a, v, b, n in sets:
        step = a.shape[0] // n
        pieces += [(a, v, b, pl.ds(i * step, step)) for i in range(n)]
    reads = [
        pltpu.make_async_copy(a.at[o], v.at[o], sem.at[0, i])
        for i, (a, v, _, o) in enumerate(pieces)
    ]
    writes = [
        pltpu.make_async_copy(v.at[o], b.at[o], sem.at[1, i])
        for i, (_, v, b, o) in enumerate(pieces)
    ]
    for c in reads:
        c.start()
    for r, w in zip(reads, writes):
        r.wait()
        w.start()
    for c in writes:
        c.wait()


def shards(tokens_in, grad_out, gate_pre, up_pre, gate_weight, up_weight, down_weight):
    scale = 1.0 / math.sqrt(4096.0)
    dma = pltpu.SemaphoreType.DMA
    vm = pltpu.VMEM
    hbm = pl.BlockSpec(memory_space=pl.ANY)
    vmem = pl.BlockSpec(memory_space=pltpu.VMEM)
    outs = pl.pallas_call(
        functools.partial(kernel, scale),
        out_shape=[
            jax.ShapeDtypeStruct((128, 1024), BF),
            jax.ShapeDtypeStruct((256, 1792), BF),
            jax.ShapeDtypeStruct((256, 1792), BF),
            jax.ShapeDtypeStruct((1792, 256), BF),
        ],
        in_specs=[hbm] * 7,
        out_specs=[hbm] * 4,
        scratch_shapes=[
            vm((128, 1024), BF),
            vm((256, 1792), BF),
            vm((256, 1792), BF),
            vm((1792, 256), BF),
            vm((1024, 1024), BF),
            vm((2, 2, 256, 1024), BF),
            vm((1792, 1024), BF),
            vm((NC, 1024, 2 * CH), BF),
            vm((NC, 4, 2, 256, CH), BF),
            vm((NC, 256, CH), BF),
            vm((NC, 2, 128, CH), BF),
            vm((NC, 2, 256, CH), BF),
            vm((NC, 2, 256, CH), BF),
            vm((2, 256, CH), F32),
            vm((2, 256, CH), F32),
            vm((NC, 4, 256, CH), BF),
            vm((1024, 2 * CH), BF),
            vm((1024, CH), BF),
            vm((2, 2, 256, 1024), BF),
            vm((1024, 1024), F32),
            vm((1024, 1024), BF),
            vm((2, 2, 64, 1024), BF),
            vm((2, 2, 2, 64, 1024), BF),
            vm((128, 1024), BF),
            vm((128, 1024), BF),
            vm((2, 2, 256, 3 * CH), BF),
            vm((NC, 2, 256, 3 * CH), BF),
            vm((2, 256, 3 * CH), F32),
            vm((2, 256, 3 * CH), BF),
            vm((NC, 256, 3 * CH), BF),
            vm((2, 256, 3 * CH), F32),
            dma((32,)),
            dma((9,)), dma((9,)),
            dma((2, 4)), dma((8,)),
            dma((3,)), dma((3,)),
            dma((NC, 3)), dma((NC, 3)),
            dma((NC, 4)), dma((NC, 4)),
            dma((NC, 2)), dma((NC, 2)),
            dma((NC, 2)), dma((NC, 2)),
            dma((NC, 2)), dma((NC, 2)),
            dma((NC, 2)), dma((NC, 2)),
            dma((NC,)), dma((NC,)),
            dma((NC,)), dma((NC,)),
            dma((2, 6)), dma((2, 6)),
            dma, dma,
            dma((NC, 3)),
        ],
        compiler_params=pltpu.CompilerParams(
            collective_id=0, has_side_effects=True, vmem_limit_bytes=62 * 2**20
        ),
        cost_estimate=pl.CostEstimate(
            flops=22_500_000_000, bytes_accessed=20_000_000, transcendentals=2_000_000
        ),
        name="swiglu_backward",
    )(tokens_in, grad_out, gate_pre, up_pre, gate_weight, up_weight, down_weight)
    return tuple(
        pl.pallas_call(
            copy_kernel,
            out_shape=[jax.ShapeDtypeStruct(o.shape, o.dtype) for o in outs],
            in_specs=[hbm] * 4,
            out_specs=[hbm] * 4,
            scratch_shapes=[*(vm(o.shape, o.dtype) for o in outs), dma((2, 13))],
            name="write_outputs",
        )(*outs)
    )


def solution(mesh):
    return jax.shard_map(
        shards,
        mesh=mesh,
        in_specs=(
            P(("depth", "row"), "col"),
            P(("depth", "row"), "col"),
            P(("depth", "col"), "row"),
            P(("depth", "col"), "row"),
            P(("col", "depth"), "row"),
            P(("col", "depth"), "row"),
            P("row", ("col", "depth")),
        ),
        out_specs=(
            P(("depth", "row"), "col"),
            P(("col", "depth"), "row"),
            P(("col", "depth"), "row"),
            P("row", ("col", "depth")),
        ),
        check_vma=False,
    )
```
